32 devices in a mesh: dom: 4 (over y, x), depth: 8 (over z, core).
Axes of the slice: x: 2, y: 2, z: 4, core: 2. Of those that a mesh axis runs over, the one named last changes fastest.
Arguments:
- head: float32 [8, 256, 512], P('depth', 'dom'), may hold values from -1.5 to 0.3
- water_prev: float32 [8, 256, 512], P('depth', 'dom'), may hold values from 0.05 to 0.4
- alpha: float32 [8, 256, 512], P('depth', 'dom'), may hold values from 0.3 to 3
- shape_n: float32 [8, 256, 512], P('depth', 'dom'), may hold values from 1.3 to 3
- theta_r: float32 [8, 256, 512], P('depth', 'dom'), may hold values from 0.02 to 0.1
- theta_s: float32 [8, 256, 512], P('depth', 'dom'), may hold values from 0.35 to 0.5
- sat_cond: float32 [8, 256, 512], P('depth', 'dom'), may hold values from 0.5 to 5
- refine: int32 [256], P('dom'), may hold values from 0 to 8
- destination: int32 [256], P('dom'), may hold values from 0 to 255, as said below
- neighbours: int32 [256, 4, 4], P('dom'), may hold values from -1 to 255, as said below
Outputs:
- new_head: float32 [8, 256, 512], P('depth', 'dom')
- residual: float32 [8, 256, 512], P('depth', 'dom')
The draws below stay inside these ranges and needn't reach their ends.
Inputs may be any that keep to these rules, and one draw needn't show every extreme that they name: destination is a permutation of the 256 positions, position p on device p // 64. The blocks of each device go to exactly 3 other devices, exactly 4 to each; its other blocks stay on it. neighbours[p, f] lists the new positions beyond lateral face f of new block p: all four entries -1 where there is no neighbour; one block in entry 0 and -1 in the rest for a face of equal size; or four finer blocks, entry (a // 4) * 2 + b // 4 for face cell (a, b). Every listed block lies at most 16 positions from p, some at exactly 16.
All inputs are finite; a program needn't handle non-finite values.
Results may differ from the reference program's by a relative error of at most 0.0003.
Values sent between devices are 32-bit elements; how exact they have to be, the bound alone decides.
A program may use at most 128 MiB of HBM per device.

```python
import math
import jax
import jax.numpy as jnp
import numpy as np
from jax import lax

CELLS = 512
BLK_DEV = 64
LAYERS = 8
BLOCKS = 256
GROUPS = 3
CAP = 4
REACH = 16


def draw_destination(key, part):
    key = jax.random.fold_in(key, 11)
    keys = jax.random.split(key, 5)
    owners = BLOCKS // BLK_DEV
    sigma = jax.random.permutation(keys[0], owners)
    inv_sigma = jnp.zeros((owners,), jnp.int32).at[sigma].set(jnp.arange(owners, dtype=jnp.int32))
    shifts = jax.random.permutation(keys[2], owners - 1)[:GROUPS] + 1
    device = jnp.arange(owners)[:, None]
    local = jnp.arange(BLK_DEV)[None, :]
    group = jnp.minimum(local // CAP, GROUPS - 1)
    moving = local < GROUPS * CAP
    target = jnp.where(moving, sigma[(inv_sigma[device] + shifts[group]) % owners], device)
    slot = jnp.broadcast_to(local, (owners, BLK_DEV))
    order = jax.vmap(lambda inner: jax.random.permutation(inner, BLK_DEV))(jax.random.split(keys[3], owners))
    place = target * BLK_DEV + order[target, slot]
    shuffle = jax.vmap(lambda inner: jax.random.permutation(inner, BLK_DEV))(jax.random.split(keys[4], owners))
    source = device * BLK_DEV + shuffle
    return jnp.zeros((BLOCKS,), jnp.int32).at[source.reshape(-1)].set(place.reshape(-1).astype(jnp.int32))


def draw_neighbours(key, part):
    key = jax.random.fold_in(key, 12)
    keys = jax.random.split(key, 3)
    position = jnp.arange(BLOCKS)[:, None, None]
    face = jnp.arange(4)[None, :, None]
    entry = jnp.arange(4)[None, None, :]
    kind = jax.random.randint(keys[0], (BLOCKS, 4, 1), 0, 10)
    sign = jax.random.randint(keys[1], (BLOCKS, 4, 4), 0, 2) * 2 - 1
    offset = jax.random.randint(keys[2], (BLOCKS, 4, 4), 1, REACH + 1) * sign
    forced = (position % BLK_DEV == BLK_DEV // 2) & (face == 1)
    offset = jnp.where(forced, REACH, offset)
    kind = jnp.where(forced, 1, kind)
    ahead = position + offset
    ahead = jnp.where((ahead < 0) | (ahead >= BLOCKS), position - offset, ahead)
    live = (kind >= 1) & ((kind >= 7) | (entry == 0))
    table = jnp.where(live, ahead, -1)
    table = table.at[0, 0].set(jnp.full((4,), -1, jnp.int32))
    table = table.at[BLOCKS - 2, 1].set(jnp.array([BLOCKS - 1, -1, -1, -1], jnp.int32))
    return table.astype(jnp.int32)


def with_ends(result, stream_key, smallest, top_value):
    longest = result.shape.index(max(result.shape))
    spots = []
    for shift in (0, 1):
        where = [jax.random.randint(jax.random.fold_in(stream_key, axis), (), 0, length) for axis, length in enumerate(result.shape)]
        where[longest] = (where[longest] + shift) % result.shape[longest]
        spots.append(tuple(where))
    return result.at[spots[0]].set(smallest).at[spots[1]].set(top_value)


def block_levels(key, shape, shards, low, high):
    loudness = 1.0
    for dim, shards_of in shards:
        steps = jax.random.uniform(jax.random.fold_in(jax.random.fold_in(key, 6), dim), (shards_of,), jnp.float32, low / len(shards), high / len(shards))
        loudness = loudness * jnp.repeat(jnp.exp(steps), shape[dim] // shards_of).reshape((-1,) + (1,) * (len(shape) - 1 - dim))
    return loudness


def setup_inputs(seed: int = 0) -> dict:
    arg_keys = jax.random.split(jax.random.key(seed), 11)
    head = jnp.clip(-1.5 + 1.8 * jax.random.uniform(arg_keys[0], (LAYERS, BLOCKS, CELLS), jnp.float32) ** block_levels(arg_keys[0], (LAYERS, BLOCKS, CELLS), ((0, 8), (1, 4)), -0.2, 0.2), -1.5, 0.3)
    water_prev = jnp.clip(0.05 + 0.35 * jax.random.uniform(arg_keys[1], (LAYERS, BLOCKS, CELLS), jnp.float32) ** block_levels(arg_keys[1], (LAYERS, BLOCKS, CELLS), ((0, 8), (1, 4)), -0.2, 0.2), 0.05, 0.4)
    alpha = jnp.clip(jnp.exp(math.log(3.0) - 2.3025851 * jax.random.uniform(arg_keys[2], (LAYERS, BLOCKS, CELLS), jnp.float32) ** block_levels(arg_keys[2], (LAYERS, BLOCKS, CELLS), ((0, 8), (1, 4)), -0.2, 0.2)), 0.3, 3.0)
    shape_n = jnp.clip(1.3 + 1.7 * jax.random.uniform(arg_keys[3], (LAYERS, BLOCKS, CELLS), jnp.float32) ** block_levels(arg_keys[3], (LAYERS, BLOCKS, CELLS), ((0, 8), (1, 4)), -0.2, 0.2), 1.3, 3.0)
    theta_r = jnp.clip(0.02 + 0.08 * jax.random.uniform(arg_keys[4], (LAYERS, BLOCKS, CELLS), jnp.float32) ** block_levels(arg_keys[4], (LAYERS, BLOCKS, CELLS), ((0, 8), (1, 4)), -0.2, 0.2), 0.02, 0.1)
    theta_s = jnp.clip(0.35 + 0.15 * jax.random.uniform(arg_keys[5], (LAYERS, BLOCKS, CELLS), jnp.float32) ** block_levels(arg_keys[5], (LAYERS, BLOCKS, CELLS), ((0, 8), (1, 4)), -0.2, 0.2), 0.35, 0.5)
    sat_cond = jnp.clip(jnp.exp(math.log(5.0) - 2.3025851 * jax.random.uniform(arg_keys[6], (LAYERS, BLOCKS, CELLS), jnp.float32) ** block_levels(arg_keys[6], (LAYERS, BLOCKS, CELLS), ((0, 8), (1, 4)), -0.2, 0.2)), 0.5, 5.0)
    refine = with_ends(jax.random.randint(arg_keys[7], (BLOCKS,), 0, 9), jax.random.fold_in(arg_keys[7], 1), 0, 8).astype(jnp.int32)
    destination = draw_destination(jax.random.fold_in(arg_keys[10], 71), 0)
    neighbours = draw_neighbours(jax.random.fold_in(arg_keys[10], 71), 0)
    return {"head": head, "water_prev": water_prev, "alpha": alpha, "shape_n": shape_n, "theta_r": theta_r, "theta_s": theta_s, "sat_cond": sat_cond, "refine": refine, "destination": destination, "neighbours": neighbours}


inv_step = 4.0

def line_tables(bit):
    low_index = []
    high_index = []
    low_weight = []
    high_weight = []
    for fine in range(8):
        half = fine // 2
        if fine % 2 == 0:
            low_index.append(max(4 * bit + half - 1, 0))
            high_index.append(4 * bit + half)
            low_weight.append(0.25)
            high_weight.append(0.75)
        else:
            low_index.append(4 * bit + half)
            high_index.append(min(4 * bit + half + 1, 7))
            low_weight.append(0.75)
            high_weight.append(0.25)
    return (np.array(low_index), np.array(high_index), np.array(low_weight, np.float32), np.array(high_weight, np.float32))

def along(cube, axis_pos, bits, smooth):
    shape = [1, 1, 1, 1, 1]
    shape[axis_pos] = 8
    results = []
    for bit in range(2):
        low_index, high_index, low_weight, high_weight = line_tables(bit)
        if smooth:
            value = jnp.take(cube, low_index, axis=axis_pos) * low_weight.reshape(shape) + jnp.take(cube, high_index, axis=axis_pos) * high_weight.reshape(shape)
        else:
            value = jnp.take(cube, np.array([4 * bit + fine // 2 for fine in range(8)]), axis=axis_pos)
        results.append(value)
    chosen = bits.reshape(1, -1, 1, 1, 1) == 1
    return jnp.where(chosen, results[1], results[0])

def adapt(fields, flags, smooth):
    octant = jnp.maximum(flags - 1, 0)
    cube = fields.reshape(fields.shape[0], fields.shape[1], 8, 8, 8)
    cube = along(cube, 2, octant // 4, smooth)
    cube = along(cube, 3, octant // 2 % 2, smooth)
    cube = along(cube, 4, octant % 2, smooth)
    return jnp.where((flags == 0).reshape(1, -1, 1), fields, cube.reshape(fields.shape))

def closure(head_cell, cell_alpha, cell_shape, cell_resid, cell_sat, cell_cond):
    expo = 1.0 - 1.0 / cell_shape
    ratio = jnp.power(cell_alpha * jnp.maximum(-head_cell, 0.0), cell_shape)
    saturation = jnp.power(1.0 + ratio, -expo)
    water = cell_resid + (cell_sat - cell_resid) * saturation
    inner = 1.0 - jnp.power(ratio / (1.0 + ratio), expo)
    conduct = cell_cond * jnp.sqrt(saturation) * inner * inner
    return (water, conduct)

def lateral_faces(cells):
    cube = cells.reshape(-1, 8, 8, 8)
    return jnp.stack([cube[:, 0], cube[:, 7], cube[:, :, 0], cube[:, :, 7]], axis=1).reshape(-1, 4, 64)

def quad_table():
    table = np.zeros((64, 4), np.int32)
    for first in range(8):
        for second in range(8):
            quarter = first // 4 * 2 + second // 4
            for pair in range(4):
                table[first * 8 + second, pair] = quarter * 64 + (2 * (first % 4) + pair // 2) * 8 + 2 * (second % 4) + pair % 2
    return table

def ghost_values(source, table_nb):
    blocks = table_nb.shape[0]
    safe = jnp.maximum(table_nb, 0)
    opposite = np.array([1, 0, 3, 2]).reshape(1, 4, 1)
    picked = source[safe, opposite]
    conform = picked[:, :, 0]
    spread = picked.transpose(0, 1, 3, 2, 4).reshape(blocks, 4, 2, 256)
    finer = jnp.take(spread, quad_table().reshape(-1), axis=3).reshape(blocks, 4, 2, 64, 4)
    hanging = 0.25 * (finer[..., 0] + finer[..., 1] + finer[..., 2] + finer[..., 3])
    count = lax.optimization_barrier(jnp.sum((table_nb >= 0).astype(jnp.int32), axis=2))
    value = jnp.where((count == 4)[:, :, None, None], hanging, conform)
    present = (count > 0).astype(jnp.float32)
    return (value, present)

def beside(cube, plane, axis_pos, first):
    plane = jnp.expand_dims(plane, axis_pos)
    if first:
        return jnp.concatenate([plane, lax.slice_in_dim(cube, 0, 7, axis=axis_pos)], axis=axis_pos)
    return jnp.concatenate([lax.slice_in_dim(cube, 1, 8, axis=axis_pos), plane], axis=axis_pos)

def balance(head_cell, water, conduct, prior, cell_alpha, cell_resid, cell_sat, lat_value, lat_on, below, above, low_on, high_on):
    blocks = head_cell.shape[0]
    cube_h = head_cell.reshape(blocks, 8, 8, 8)
    cube_k = conduct.reshape(blocks, 8, 8, 8)
    ones = jnp.ones_like(cube_h)
    flux = jnp.zeros_like(cube_h)
    total = jnp.zeros_like(cube_h)
    plans = []
    for face, axis_pos, first in ((0, 1, True), (1, 1, False), (2, 2, True), (3, 2, False)):
        plane_on = ones[:, 0] * lat_on[:, face].reshape(blocks, 1, 1)
        plans.append((lat_value[:, face, 0].reshape(blocks, 8, 8), lat_value[:, face, 1].reshape(blocks, 8, 8), plane_on, axis_pos, first, 0.0))
    plans.append((below[:, 0].reshape(blocks, 8, 8), below[:, 1].reshape(blocks, 8, 8), ones[:, 0] * low_on, 3, True, -1.0))
    plans.append((above[:, 0].reshape(blocks, 8, 8), above[:, 1].reshape(blocks, 8, 8), ones[:, 0] * high_on, 3, False, 1.0))
    for plane_h, plane_k, plane_on, axis_pos, first, lift in plans:
        near_h = beside(cube_h, plane_h, axis_pos, first)
        near_k = beside(cube_k, plane_k, axis_pos, first)
        near_on = beside(ones, plane_on, axis_pos, first)
        face_k = near_on * 0.5 * (cube_k + near_k)
        flux = flux + face_k * (near_h - cube_h + lift)
        total = total + face_k
    resid = inv_step * (water - prior) - flux.reshape(blocks, -1)
    diagonal = inv_step * (cell_sat - cell_resid) * cell_alpha + total.reshape(blocks, -1)
    return (resid, diagonal)

def planes(cells, conduct, level_k):
    layers, blocks = (cells.shape[0], cells.shape[1])
    plane_h = cells.reshape(layers, blocks, 8, 8, 8)[..., level_k].reshape(layers, blocks, 64)
    plane_k = conduct.reshape(layers, blocks, 8, 8, 8)[..., level_k].reshape(layers, blocks, 64)
    return jnp.stack([plane_h, plane_k], axis=2)

def evaluate(head_all, prior, cell_alpha, cell_shape, cell_resid, cell_sat, cell_cond, neighbours):
    water, conduct = closure(head_all, cell_alpha, cell_shape, cell_resid, cell_sat, cell_cond)
    layers = head_all.shape[0]
    bottoms = planes(head_all, conduct, 0)
    tops = planes(head_all, conduct, 7)
    empty = jnp.zeros_like(tops[:1])
    below = jnp.concatenate([empty, tops[:-1]], axis=0)
    above = jnp.concatenate([bottoms[1:], empty], axis=0)
    level = jnp.arange(layers)
    low_on = (level > 0).astype(jnp.float32)
    high_on = (level < layers - 1).astype(jnp.float32)

    def one_layer(items):
        head_l, water_l, cond_l, prior_l, alpha_l, resid_l, sat_l, below_l, above_l, low_l, high_l = items
        faces = jnp.stack([lateral_faces(head_l), lateral_faces(cond_l)], axis=2)
        lat_value, lat_on = ghost_values(faces, neighbours)
        return balance(head_l, water_l, cond_l, prior_l, alpha_l, resid_l, sat_l, lat_value, lat_on, below_l, above_l, low_l, high_l)
    return lax.map(one_layer, (head_all, water, conduct, prior, cell_alpha, cell_resid, cell_sat, below, above, low_on, high_on))

def reference(head, water_prev, alpha, shape_n, theta_r, theta_s, sat_cond, refine, destination, neighbours):
    adapted = [adapt(field, refine, True) for field in (head, water_prev)]
    adapted = adapted + [adapt(field, refine, False) for field in (alpha, shape_n, theta_r, theta_s, sat_cond)]
    moved = [jnp.zeros_like(field).at[:, destination].set(field) for field in adapted]
    start, prior, cell_alpha, cell_shape, cell_resid, cell_sat, cell_cond = moved
    resid, diagonal = evaluate(start, prior, cell_alpha, cell_shape, cell_resid, cell_sat, cell_cond, neighbours)
    new_head = start - resid / diagonal
    final, unused = evaluate(new_head, prior, cell_alpha, cell_shape, cell_resid, cell_sat, cell_cond, neighbours)
    return (new_head, final)
```

```python
import functools

import jax
import jax.numpy as jnp
import numpy as np
from jax import lax
from jax.experimental import pallas as pl
from jax.experimental.pallas import tpu as pltpu
from jax.sharding import PartitionSpec as P

MESH = pl.DeviceIdType.MESH
CELLS = 512
CAP = 4
REACH = 16
F32 = jnp.float32
BF16 = jnp.bfloat16


def face_cells(face):
    listed = []
    for first in range(8):
        for second in range(8):
            listed.append(
                (
                    first * 8 + second,
                    448 + first * 8 + second,
                    first * 64 + second,
                    first * 64 + 56 + second,
                    first * 64 + second * 8,
                    first * 64 + second * 8 + 7,
                )[face]
            )
    return listed


def take_table():
    table = np.zeros((CELLS, 384), np.float32)
    for face in range(6):
        for spot, cell in enumerate(face_cells(face)):
            table[cell, face * 64 + spot] = 1.0
    return table


def pool_table():
    table = np.zeros((128, 128), np.float32)
    for half in range(2):
        for a in range(8):
            for b in range(8):
                for u in range(2):
                    for w in range(2):
                        source = (2 * (a % 4) + u) * 8 + 2 * (b % 4) + w
                        table[half * 64 + source, half * 64 + a * 8 + b] = 0.25
    return table


def iota(shape, axis):
    return lax.broadcasted_iota(jnp.int32, shape, axis)


def split(x):
    high = x.astype(BF16)
    return high, (x - high.astype(F32)).astype(BF16)


def dot(a, b):
    return jnp.dot(a, b, preferred_element_type=F32)


def lanes_of(x, index):
    return jnp.take_along_axis(x, index, axis=1, mode="promise_in_bounds")


def adapt_rows(load, store, flags):
    rows = flags.shape[0]
    shape = (rows, 128)
    flag = jnp.broadcast_to(flags, shape)
    octant = jnp.maximum(flag - 1, 0)
    kept = flag == 0
    bx = (octant >> 2) == 1
    by = (octant >> 1) & 1
    bz = octant & 1
    lane = iota(shape, 1)
    y = (lane >> 3) & 7
    z = lane & 7
    half = lane & 64
    low = lane < 64
    ya = 4 * by + (y >> 1)
    za = 4 * bz + (z >> 1)
    yb = jnp.clip(ya + 2 * (y & 1) - 1, 0, 7)
    zb = jnp.clip(za + 2 * (z & 1) - 1, 0, 7)
    index_ya = half + ya * 8 + z
    index_yb = half + yb * 8 + z
    index_za = half + y * 8 + za
    index_zb = half + y * 8 + zb
    index_plain = ya * 8 + za
    v = [load(0, j) for j in range(4)]
    w = [pltpu.roll(chunk, 64, 1) for chunk in v]
    v0 = jnp.where(bx, v[2], v[0])
    v1 = jnp.where(bx, v[3], v[1])
    w0 = jnp.where(bx, w[2], w[0])
    w1 = jnp.where(bx, w[3], w[1])
    before = jnp.where(bx, w[1], v[0])
    after = jnp.where(bx, v[3], w[2])
    near = (
        jnp.where(low, v0, w0),
        jnp.where(low, w0, v0),
        jnp.where(low, v1, w1),
        jnp.where(low, w1, v1),
    )
    far = (
        jnp.where(low, before, v0),
        jnp.where(low, v0, w1),
        jnp.where(low, w0, v1),
        jnp.where(low, v1, after),
    )
    for j in range(4):
        cur = 0.75 * near[j] + 0.25 * far[j]
        cur = 0.75 * lanes_of(cur, index_ya) + 0.25 * lanes_of(cur, index_yb)
        cur = 0.75 * lanes_of(cur, index_za) + 0.25 * lanes_of(cur, index_zb)
        store(0, j, jnp.where(kept, v[j], cur))
    for s in range(1, 4):
        v = [load(s, j) for j in range(4)]
        for j in range(4):
            source = jnp.where(bx, v[2 + j // 2], v[j // 2])
            cur = lanes_of(source, index_plain + (j % 2) * 64)
            store(s, j, jnp.where(kept, v[j], cur))


def kernel(
    peers,
    layers,
    head,
    water_prev,
    alpha,
    shape_n,
    theta_r,
    theta_s,
    sat_cond,
    refine,
    destination,
    neighbours,
    t_take,
    t_put,
    t_pool,
    new_head,
    residual,
    raw,
    sent,
    got,
    work,
    settled,
    got_work,
    place,
    fine_hot,
    pool_hot,
    present,
    faces,
    planes,
    halo,
    ghost_planes,
    fields,
    move_send,
    move_recv,
    halo_send,
    halo_recv,
    plane_send,
    plane_recv,
):
    me = lax.axis_index("dom")
    level = lax.axis_index("depth")
    blocks = head.shape[1]
    both = 2 * blocks
    slots = 8 * peers
    shift = blocks.bit_length() - 1

    halo[...] = jnp.zeros_like(halo)
    ghost_planes[...] = jnp.zeros_like(ghost_planes)
    got[0] = jnp.zeros(got.shape[1:], F32)

    barrier = pltpu.get_barrier_semaphore()
    for k in range(1, peers):
        pl.semaphore_signal(
            barrier, inc=1, device_id=(lax.rem(me + k, peers), level), device_id_type=MESH
        )

    @pl.when(level > 0)
    def _():
        pl.semaphore_signal(barrier, inc=1, device_id=(me, level - 1), device_id_type=MESH)

    @pl.when(level < layers - 1)
    def _():
        pl.semaphore_signal(barrier, inc=1, device_id=(me, level + 1), device_id_type=MESH)

    left = (head, alpha, shape_n, sat_cond)
    right = (water_prev, theta_r, theta_s)
    for s in range(4):
        cols = pl.ds(s * CELLS, CELLS)
        high, rest = split(left[s][0])
        raw[pl.ds(0, blocks), cols] = high
        raw[pl.ds(both, blocks), cols] = rest
        if s < 3:
            high, rest = split(right[s][0])
            raw[pl.ds(blocks, blocks), cols] = high
            raw[pl.ds(both + blocks, blocks), cols] = rest
        else:
            raw[pl.ds(blocks, blocks), cols] = jnp.zeros((blocks, CELLS), BF16)
            raw[pl.ds(both + blocks, blocks), cols] = jnp.zeros((blocks, CELLS), BF16)

    dest = jnp.concatenate([destination[...], destination[...]], axis=1)
    flag_row = jnp.concatenate([refine[...], refine[...]], axis=1)
    owner = dest >> shift
    spot = dest & (blocks - 1)
    shape = (blocks, both)
    own_lane = iota(shape, 1)
    own_row = iota(shape, 0)
    diagonal = own_lane == own_row
    owner_col = jnp.sum(jnp.where(diagonal, owner, 0), axis=1, keepdims=True)
    flag_col = jnp.sum(jnp.where(diagonal, flag_row, 0), axis=1, keepdims=True)
    earlier = (owner_col == owner) & (own_row < (own_lane & (blocks - 1)))
    rank = jnp.sum(earlier.astype(jnp.int32), axis=0, keepdims=True)
    shape = (slots, both)
    row = iota(shape, 0)
    side = (row >> 2) & 1
    target = me + (row >> 3)
    target = jnp.where(target >= peers, target - peers, target)
    chosen = (
        (side == (iota(shape, 1) >> shift))
        & (owner == target)
        & (rank == (row & 3))
        & (row >= 8)
    )
    hot = jnp.where(chosen, 1.0, 0.0)
    spot_sent = jnp.sum(hot * (spot + 1).astype(F32), axis=1, keepdims=True) - 1.0
    flag_sent = jnp.sum(hot * flag_row.astype(F32), axis=1, keepdims=True)
    hot = hot.astype(BF16)
    packed = dot(jnp.concatenate([hot, hot], axis=1), raw[...])
    sent[:, :, pl.ds(0, 4 * CELLS)] = packed.reshape(peers, 8, 4 * CELLS)
    meta = jnp.where(iota((slots, 128), 1) < 64, spot_sent, flag_sent)
    sent[:, :, pl.ds(4 * CELLS, 128)] = meta.reshape(peers, 8, 128)

    @pl.when((level > 0) & (level < layers - 1))
    def _():
        pl.semaphore_wait(barrier, peers + 1)

    @pl.when((level == 0) | (level == layers - 1))
    def _():
        pl.semaphore_wait(barrier, peers)

    moves = []
    for k in range(1, peers):
        moves.append(
            pltpu.make_async_remote_copy(
                src_ref=sent.at[k],
                dst_ref=got.at[k],
                send_sem=move_send.at[k],
                recv_sem=move_recv.at[k],
                device_id=(lax.rem(me + k, peers), level),
                device_id_type=MESH,
            )
        )
    for copy in moves:
        copy.start()

    flags16 = flag_col
    for start in range(0, both, 16):
        base = start % blocks

        def load(s, j, start=start, base=base):
            refs = left if start < blocks else right
            if s == 3 and start >= blocks:
                return jnp.zeros((16, 128), F32)
            return refs[s][0, pl.ds(base, 16), pl.ds(j * 128, 128)]

        def store(s, j, value, start=start):
            cols = pl.ds(s * CELLS + j * 128, 128)
            high, rest = split(value)
            work[pl.ds(start, 16), cols] = high
            work[pl.ds(both + start, 16), cols] = rest

        adapt_rows(load, store, flags16[base : base + 16])
    shape = (both, both)
    wanted = (
        (iota(shape, 0) - spot == ((iota(shape, 0) >> shift) << shift))
        & ((iota(shape, 0) >> shift) == (iota(shape, 1) >> shift))
        & (owner == me)
    )
    hot = jnp.where(wanted, 1.0, 0.0).astype(BF16)
    settled[...] = dot(jnp.concatenate([hot, hot], axis=1), work[...])

    first_row = me * blocks - REACH
    shape = (blocks, 128)
    lane = iota(shape, 1)
    low = lane < 64
    quarter = ((lane >> 5) & 1) * 2 + ((lane >> 2) & 1)
    for chunk in range(2):
        counts = []
        for pair in range(2):
            face = chunk * 2 + pair
            entry = [neighbours[:, pl.ds(face * 4 + e, 1)] for e in range(4)]
            full = entry[3] >= 0
            for e in range(4):
                hot = (lane == entry[e] - first_row) & (entry[e] >= 0)
                rows = pl.ds((pair * 4 + e) * blocks, blocks)
                value = jnp.where(hot & full, 1.0, 0.0).astype(BF16)
                pool_hot[chunk, rows, pl.ds(0, 128)] = value
                pool_hot[chunk, rows, pl.ds(128, 128)] = value
                if e == 0:
                    rows = pl.ds(pair * blocks, blocks)
                    value = jnp.where(hot & jnp.logical_not(full), 1.0, 0.0).astype(BF16)
                    fine_hot[chunk, rows, pl.ds(0, 128)] = value
                    fine_hot[chunk, rows, pl.ds(128, 128)] = value
            counts.append(jnp.where(entry[0] >= 0, 0.5, 0.0))
        present[:, pl.ds(chunk * 128, 128)] = jnp.where(low, counts[0], counts[1])
    low_on = jnp.where(level > 0, 0.5, 0.0)
    high_on = jnp.where(level < layers - 1, 0.5, 0.0)
    present[:, pl.ds(256, 128)] = jnp.where(low, low_on, high_on)
    lift = jnp.where(low, -1.0, 1.0)

    for copy in moves:
        copy.wait()

    meta = got[:, :, pl.ds(4 * CELLS, 128)].reshape(slots, 128)
    spot_got = meta[:, :1]
    flag_got = meta[:, 64:65].astype(jnp.int32)
    shape = (slots, both)
    row = iota(shape, 0)
    used = (
        ((iota(shape, 1) & (blocks - 1)).astype(F32) == spot_got)
        & ((iota(shape, 1) >> shift) == ((row >> 2) & 1))
        & (row >= 8)
    )
    hot = jnp.where(used, 1.0, 0.0).astype(BF16)
    for start in range(0, slots, 16):

        def load(s, j, start=start):
            return got[
                pl.ds(start // 8, 2), :, pl.ds(s * CELLS + j * 128, 128)
            ].reshape(16, 128)

        def store(s, j, value, start=start):
            cols = pl.ds(s * CELLS + j * 128, 128)
            high, rest = split(value)
            got_work[pl.ds(start, 16), cols] = high
            got_work[pl.ds(slots + start, 16), cols] = rest

        adapt_rows(load, store, flag_got[start : start + 16])
    hot = jnp.concatenate([hot, hot], axis=0)
    settled[...] += lax.dot_general(
        hot, got_work[...], (((0,), (0,)), ((), ())), preferred_element_type=F32
    )

    top_rows = pl.ds(0, blocks)
    end_rows = pl.ds(blocks, blocks)
    seg = [pl.ds(s * CELLS, CELLS) for s in range(4)]

    def closure(h):
        n = settled[top_rows, seg[2]]
        m = 1.0 - 1.0 / n
        log_x = jnp.log(settled[top_rows, seg[1]] * jnp.maximum(-h, 0.0))
        log_up = m * jnp.log(1.0 + jnp.exp(n * log_x))
        root = jnp.exp(-0.5 * log_up)
        inner = 1.0 - jnp.exp((n - 1.0) * log_x - log_up)
        resid = settled[end_rows, seg[1]]
        water = resid + (settled[end_rows, seg[2]] - resid) * root * root
        conduct = settled[top_rows, seg[3]] * root * inner * inner
        return water, conduct

    lane_all = iota((blocks, CELLS), 1)

    def evaluate(step, h, diag):
        water, conduct = closure(h)
        terms = jnp.concatenate([*split(h), *split(conduct)], axis=0)
        taken = dot(terms, t_take[...])
        face_h = taken[:blocks] + taken[blocks:both]
        face_k = taken[both : both + blocks] + taken[both + blocks :]
        faces[0] = face_h[:, :256]
        faces[1] = face_k[:, :256]
        edge_h = face_h[:, 256:]
        edge_k = face_k[:, 256:]
        planes[0] = jnp.where(low, edge_h, pltpu.roll(edge_k, 64, 1))
        planes[1] = jnp.where(low, pltpu.roll(edge_h, 64, 1), edge_k)

        def halo_copy(side, way):
            start = 0 if side else blocks - REACH
            return pltpu.make_async_remote_copy(
                src_ref=faces.at[:, pl.ds(start, REACH)],
                dst_ref=halo.at[step, side],
                send_sem=halo_send.at[step, side],
                recv_sem=halo_recv.at[step, side],
                device_id=(me + way, level),
                device_id_type=MESH,
            )

        def plane_copy(side, way):
            return pltpu.make_async_remote_copy(
                src_ref=planes.at[1 - side],
                dst_ref=ghost_planes.at[step, side],
                send_sem=plane_send.at[step, side],
                recv_sem=plane_recv.at[step, side],
                device_id=(me, level + way),
                device_id_type=MESH,
            )

        @pl.when(me < peers - 1)
        def _():
            halo_copy(0, 1).start()

        @pl.when(me > 0)
        def _():
            halo_copy(1, -1).start()

        @pl.when(level < layers - 1)
        def _():
            plane_copy(0, 1).start()

        @pl.when(level > 0)
        def _():
            plane_copy(1, -1).start()

        flux = jnp.zeros((blocks, CELLS), F32)
        total = jnp.zeros((blocks, CELLS), F32)
        for stride, rise in ((64, 0.0), (8, 0.0), (1, 1.0)):
            inside = ((lane_all // stride) & 7) < 7
            near_h = pltpu.roll(h, CELLS - stride, 1)
            near_k = pltpu.roll(conduct, CELLS - stride, 1)
            part = jnp.where(inside, 0.5 * (conduct + near_k), 0.0)
            gain = part * (near_h - h + rise)
            flux = flux + gain - pltpu.roll(gain, stride, 1)
            if diag:
                total = total + part + pltpu.roll(part, stride, 1)
        fields[0] = 4.0 * (water - settled[end_rows, seg[0]]) - flux
        if diag:
            resid = settled[end_rows, seg[1]]
            fields[1] = (
                4.0 * (settled[end_rows, seg[2]] - resid) * settled[top_rows, seg[1]] + total
            )

        @pl.when(me < peers - 1)
        def _():
            halo_copy(0, 1).wait_send()
            halo_copy(1, -1).wait_recv()

        @pl.when(me > 0)
        def _():
            halo_copy(1, -1).wait_send()
            halo_copy(0, 1).wait_recv()

        @pl.when(level < layers - 1)
        def _():
            plane_copy(0, 1).wait_send()
            plane_copy(1, -1).wait_recv()

        @pl.when(level > 0)
        def _():
            plane_copy(1, -1).wait_send()
            plane_copy(0, 1).wait_recv()

        spare = jnp.zeros((128 - blocks - 2 * REACH, 128), F32)
        out_h = []
        out_k = []
        for chunk in range(2):
            cols = pl.ds(chunk * 128, 128)
            terms = []
            for kind in range(2):
                wide = jnp.concatenate(
                    [halo[step, 0, kind, :, cols], faces[kind, :, cols], halo[step, 1, kind, :, cols], spare],
                    axis=0,
                )
                terms.append(jnp.concatenate(split(wide), axis=0))
            pooled = dot(jnp.concatenate(terms, axis=0), t_pool[...])
            pooled = [pooled[:128] + pooled[128:256], pooled[256:384] + pooled[384:]]
            pooled = [jnp.concatenate(split(x), axis=0) for x in pooled]
            fine = dot(fine_hot[chunk], jnp.concatenate(terms, axis=1))
            pool = dot(pool_hot[chunk], jnp.concatenate(pooled, axis=1))
            for kind, out in ((0, out_h), (1, out_k)):
                col = slice(kind * 128, kind * 128 + 128)
                sides = []
                for pair in range(2):
                    quad = [
                        pool[(pair * 4 + e) * blocks : (pair * 4 + e + 1) * blocks, col]
                        for e in range(4)
                    ]
                    hanging = jnp.where(
                        quarter < 2,
                        jnp.where(quarter == 0, quad[0], quad[1]),
                        jnp.where(quarter == 2, quad[2], quad[3]),
                    )
                    sides.append(hanging + fine[pair * blocks : (pair + 1) * blocks, col])
                out.append(pltpu.roll(jnp.where(low, sides[1], sides[0]), 64, 1))
        below = ghost_planes[step, 0]
        above = ghost_planes[step, 1]
        out_h.append(jnp.where(low, below, pltpu.roll(above, 64, 1)) + lift)
        out_k.append(jnp.where(low, pltpu.roll(below, 64, 1), above))
        rim = present[...] * (face_k + jnp.concatenate(out_k, axis=1))
        push = rim * (jnp.concatenate(out_h, axis=1) - face_h)
        if diag:
            spread = dot(jnp.concatenate([*split(push), *split(rim)], axis=0), t_put[...])
            resid = fields[0] - (spread[:blocks] + spread[blocks:both])
            return resid, fields[1] + spread[both : both + blocks] + spread[both + blocks :]
        spread = dot(jnp.concatenate(split(push), axis=0), t_put[...])
        return fields[0] - (spread[:blocks] + spread[blocks:]), None

    start_head = settled[top_rows, seg[0]]
    resid, diag = evaluate(0, start_head, True)
    fresh = start_head - resid / diag
    new_head[0] = fresh
    resid, _ = evaluate(1, fresh, False)
    residual[0] = resid


def on_device(
    peers,
    layers,
    head,
    water_prev,
    alpha,
    shape_n,
    theta_r,
    theta_s,
    sat_cond,
    refine,
    destination,
    neighbours,
):
    blocks = head.shape[1]
    both = 2 * blocks
    slots = 8 * peers
    table = take_table()
    vmem = pl.BlockSpec(memory_space=pltpu.VMEM)
    dma = pltpu.SemaphoreType.DMA
    return pl.pallas_call(
        functools.partial(kernel, peers, layers),
        out_shape=(
            jax.ShapeDtypeStruct(head.shape, F32),
            jax.ShapeDtypeStruct(head.shape, F32),
        ),
        in_specs=[vmem] * 13,
        out_specs=(vmem, vmem),
        scratch_shapes=[
            pltpu.VMEM((2 * both, 4 * CELLS), BF16),
            pltpu.VMEM((peers, 8, 4 * CELLS + 128), F32),
            pltpu.VMEM((peers, 8, 4 * CELLS + 128), F32),
            pltpu.VMEM((2 * both, 4 * CELLS), BF16),
            pltpu.VMEM((both, 4 * CELLS), F32),
            pltpu.VMEM((2 * slots, 4 * CELLS), BF16),
            pltpu.VMEM((8, 128), F32),
            pltpu.VMEM((2, 2 * blocks, 256), BF16),
            pltpu.VMEM((2, 8 * blocks, 256), BF16),
            pltpu.VMEM((blocks, 384), F32),
            pltpu.VMEM((2, blocks, 256), F32),
            pltpu.VMEM((2, blocks, 128), F32),
            pltpu.VMEM((2, 2, 2, REACH, 256), F32),
            pltpu.VMEM((2, 2, blocks, 128), F32),
            pltpu.VMEM((2, blocks, CELLS), F32),
            dma((peers,)),
            dma((peers,)),
            dma((2, 2)),
            dma((2, 2)),
            dma((2, 2)),
            dma((2, 2)),
        ],
        compiler_params=pltpu.CompilerParams(
            collective_id=0, has_side_effects=True, vmem_limit_bytes=48 * 1024 * 1024
        ),
    )(
        head,
        water_prev,
        alpha,
        shape_n,
        theta_r,
        theta_s,
        sat_cond,
        refine.reshape(1, blocks),
        destination.reshape(1, blocks),
        neighbours.reshape(blocks, 16),
        jnp.asarray(table, BF16),
        jnp.asarray(table.T, BF16),
        jnp.asarray(pool_table(), BF16),
    )


def solution(mesh):
    cells = P("depth", "dom", None)
    placed = (cells,) * 7 + (P("dom"), P("dom"), P("dom", None, None))
    return jax.shard_map(
        functools.partial(on_device, mesh.shape["dom"], mesh.shape["depth"]),
        mesh=mesh,
        in_specs=placed,
        out_specs=(cells, cells),
        check_vma=False,
    )
```

```python
import functools

import jax
import jax.numpy as jnp
import numpy as np
from jax import lax
from jax.experimental import pallas as pl
from jax.experimental.pallas import tpu as pltpu
from jax.sharding import PartitionSpec as P

MESH = pl.DeviceIdType.MESH
CELLS = 512
CAP = 4
REACH = 16
F32 = jnp.float32
BF16 = jnp.bfloat16


def face_cells(face):
    listed = []
    for first in range(8):
        for second in range(8):
            listed.append(
                (
                    first * 8 + second,
                    448 + first * 8 + second,
                    first * 64 + second,
                    first * 64 + 56 + second,
                    first * 64 + second * 8,
                    first * 64 + second * 8 + 7,
                )[face]
            )
    return listed


def take_table():
    table = np.zeros((CELLS, 384), np.float32)
    for face in range(6):
        for spot, cell in enumerate(face_cells(face)):
            table[cell, face * 64 + spot] = 1.0
    return table


def pool_table():
    table = np.zeros((128, 128), np.float32)
    for half in range(2):
        for a in range(8):
            for b in range(8):
                for u in range(2):
                    for w in range(2):
                        source = (2 * (a % 4) + u) * 8 + 2 * (b % 4) + w
                        table[half * 64 + source, half * 64 + a * 8 + b] = 0.25
    return table


def iota(shape, axis):
    return lax.broadcasted_iota(jnp.int32, shape, axis)


def split(x):
    high = x.astype(BF16)
    return high, (x - high.astype(F32)).astype(BF16)


def dot(a, b):
    return jnp.dot(a, b, preferred_element_type=F32)


def lanes_of(x, index):
    return jnp.take_along_axis(x, index, axis=1, mode="promise_in_bounds")


def adapt_rows(load, store, flags):
    rows = flags.shape[0]
    shape = (rows, 128)
    flag = jnp.broadcast_to(flags, shape)
    octant = jnp.maximum(flag - 1, 0)
    kept = flag == 0
    bx = (octant >> 2) == 1
    by = (octant >> 1) & 1
    bz = octant & 1
    lane = iota(shape, 1)
    y = (lane >> 3) & 7
    z = lane & 7
    half = lane & 64
    low = lane < 64
    ya = 4 * by + (y >> 1)
    za = 4 * bz + (z >> 1)
    yb = jnp.clip(ya + 2 * (y & 1) - 1, 0, 7)
    zb = jnp.clip(za + 2 * (z & 1) - 1, 0, 7)
    index_ya = half + ya * 8 + z
    index_yb = half + yb * 8 + z
    index_za = half + y * 8 + za
    index_zb = half + y * 8 + zb
    index_plain = ya * 8 + za
    v = [load(0, j) for j in range(4)]
    w = [pltpu.roll(chunk, 64, 1) for chunk in v]
    v0 = jnp.where(bx, v[2], v[0])
    v1 = jnp.where(bx, v[3], v[1])
    w0 = jnp.where(bx, w[2], w[0])
    w1 = jnp.where(bx, w[3], w[1])
    before = jnp.where(bx, w[1], v[0])
    after = jnp.where(bx, v[3], w[2])
    near = (
        jnp.where(low, v0, w0),
        jnp.where(low, w0, v0),
        jnp.where(low, v1, w1),
        jnp.where(low, w1, v1),
    )
    far = (
        jnp.where(low, before, v0),
        jnp.where(low, v0, w1),
        jnp.where(low, w0, v1),
        jnp.where(low, v1, after),
    )
    for j in range(4):
        cur = 0.75 * near[j] + 0.25 * far[j]
        cur = 0.75 * lanes_of(cur, index_ya) + 0.25 * lanes_of(cur, index_yb)
        cur = 0.75 * lanes_of(cur, index_za) + 0.25 * lanes_of(cur, index_zb)
        store(0, j, jnp.where(kept, v[j], cur))
    for s in range(1, 4):
        v = [load(s, j) for j in range(4)]
        for j in range(4):
            source = jnp.where(bx, v[2 + j // 2], v[j // 2])
            cur = lanes_of(source, index_plain + (j % 2) * 64)
            store(s, j, jnp.where(kept, v[j], cur))


def kernel(
    peers,
    layers,
    head_hbm,
    water_prev_hbm,
    alpha_hbm,
    shape_n_hbm,
    theta_r_hbm,
    theta_s_hbm,
    sat_cond_hbm,
    refine_hbm,
    destination_hbm,
    neighbours_hbm,
    t_take_hbm,
    t_put_hbm,
    t_pool_hbm,
    new_head,
    residual,
    head,
    water_prev,
    alpha,
    shape_n,
    theta_r,
    theta_s,
    sat_cond,
    refine,
    destination,
    neighbours,
    t_take,
    t_put,
    t_pool,
    load_sem,
    raw,
    sent,
    got,
    work,
    settled,
    got_work,
    place,
    fine_hot,
    pool_hot,
    present,
    faces,
    planes,
    halo,
    ghost_planes,
    fields,
    move_send,
    move_recv,
    halo_send,
    halo_recv,
    plane_send,
    plane_recv,
):
    me = lax.axis_index("dom")
    level = lax.axis_index("depth")
    blocks = head.shape[1]
    both = 2 * blocks
    slots = 8 * peers
    shift = blocks.bit_length() - 1

    loads = []
    for source, target in (
        (destination_hbm, destination),
        (refine_hbm, refine),
        (head_hbm, head),
        (water_prev_hbm, water_prev),
        (alpha_hbm, alpha),
        (theta_r_hbm, theta_r),
        (shape_n_hbm, shape_n),
        (theta_s_hbm, theta_s),
        (sat_cond_hbm, sat_cond),
        (neighbours_hbm, neighbours),
        (t_take_hbm, t_take),
        (t_pool_hbm, t_pool),
        (t_put_hbm, t_put),
    ):
        loads.append(pltpu.make_async_copy(source, target, load_sem.at[len(loads)]))
    for copy in loads:
        copy.start()

    halo[...] = jnp.zeros_like(halo)
    ghost_planes[...] = jnp.zeros_like(ghost_planes)
    got[0] = jnp.zeros(got.shape[1:], F32)

    barrier = pltpu.get_barrier_semaphore()
    for k in range(1, peers):
        pl.semaphore_signal(
            barrier, inc=1, device_id=(lax.rem(me + k, peers), level), device_id_type=MESH
        )

    @pl.when(level > 0)
    def _():
        pl.semaphore_signal(barrier, inc=1, device_id=(me, level - 1), device_id_type=MESH)

    @pl.when(level < layers - 1)
    def _():
        pl.semaphore_signal(barrier, inc=1, device_id=(me, level + 1), device_id_type=MESH)

    for copy in loads[:9]:
        copy.wait()
    left = (head, alpha, shape_n, sat_cond)
    right = (water_prev, theta_r, theta_s)
    for s in range(4):
        cols = pl.ds(s * CELLS, CELLS)
        high, rest = split(left[s][0])
        raw[pl.ds(0, blocks), cols] = high
        raw[pl.ds(both, blocks), cols] = rest
        if s < 3:
            high, rest = split(right[s][0])
            raw[pl.ds(blocks, blocks), cols] = high
            raw[pl.ds(both + blocks, blocks), cols] = rest
        else:
            raw[pl.ds(blocks, blocks), cols] = jnp.zeros((blocks, CELLS), BF16)
            raw[pl.ds(both + blocks, blocks), cols] = jnp.zeros((blocks, CELLS), BF16)

    dest = jnp.concatenate([destination[...], destination[...]], axis=1)
    flag_row = jnp.concatenate([refine[...], refine[...]], axis=1)
    owner = dest >> shift
    spot = dest & (blocks - 1)
    shape = (blocks, both)
    own_lane = iota(shape, 1)
    own_row = iota(shape, 0)
    diagonal = own_lane == own_row
    owner_col = jnp.sum(jnp.where(diagonal, owner, 0), axis=1, keepdims=True)
    flag_col = jnp.sum(jnp.where(diagonal, flag_row, 0), axis=1, keepdims=True)
    earlier = (owner_col == owner) & (own_row < (own_lane & (blocks - 1)))
    rank = jnp.sum(earlier.astype(jnp.int32), axis=0, keepdims=True)
    shape = (slots, both)
    row = iota(shape, 0)
    side = (row >> 2) & 1
    target = me + (row >> 3)
    target = jnp.where(target >= peers, target - peers, target)
    chosen = (
        (side == (iota(shape, 1) >> shift))
        & (owner == target)
        & (rank == (row & 3))
        & (row >= 8)
    )
    hot = jnp.where(chosen, 1.0, 0.0)
    spot_sent = jnp.sum(hot * (spot + 1).astype(F32), axis=1, keepdims=True) - 1.0
    flag_sent = jnp.sum(hot * flag_row.astype(F32), axis=1, keepdims=True)
    hot = hot.astype(BF16)
    packed = dot(jnp.concatenate([hot, hot], axis=1), raw[...])
    sent[:, :, pl.ds(0, 4 * CELLS)] = packed.reshape(peers, 8, 4 * CELLS)
    meta = jnp.where(iota((slots, 128), 1) < 64, spot_sent, flag_sent)
    sent[:, :, pl.ds(4 * CELLS, 128)] = meta.reshape(peers, 8, 128)

    @pl.when((level > 0) & (level < layers - 1))
    def _():
        pl.semaphore_wait(barrier, peers + 1)

    @pl.when((level == 0) | (level == layers - 1))
    def _():
        pl.semaphore_wait(barrier, peers)

    moves = []
    for k in range(1, peers):
        moves.append(
            pltpu.make_async_remote_copy(
                src_ref=sent.at[k],
                dst_ref=got.at[k],
                send_sem=move_send.at[k],
                recv_sem=move_recv.at[k],
                device_id=(lax.rem(me + k, peers), level),
                device_id_type=MESH,
            )
        )
    for copy in moves:
        copy.start()

    flags16 = flag_col
    for start in range(0, both, 16):
        base = start % blocks

        def load(s, j, start=start, base=base):
            refs = left if start < blocks else right
            if s == 3 and start >= blocks:
                return jnp.zeros((16, 128), F32)
            return refs[s][0, pl.ds(base, 16), pl.ds(j * 128, 128)]

        def store(s, j, value, start=start):
            cols = pl.ds(s * CELLS + j * 128, 128)
            high, rest = split(value)
            work[pl.ds(start, 16), cols] = high
            work[pl.ds(both + start, 16), cols] = rest

        adapt_rows(load, store, flags16[base : base + 16])
    shape = (both, both)
    wanted = (
        (iota(shape, 0) - spot == ((iota(shape, 0) >> shift) << shift))
        & ((iota(shape, 0) >> shift) == (iota(shape, 1) >> shift))
        & (owner == me)
    )
    hot = jnp.where(wanted, 1.0, 0.0).astype(BF16)
    settled[...] = dot(jnp.concatenate([hot, hot], axis=1), work[...])

    for copy in loads[9:]:
        copy.wait()
    first_row = me * blocks - REACH
    eye = jnp.where(iota((blocks, blocks), 0) == iota((blocks, blocks), 1), 1.0, 0.0)
    shape = (blocks, 128)
    lane = iota(shape, 1)
    low = lane < 64
    quarter = ((lane >> 5) & 1) * 2 + ((lane >> 2) & 1)
    for chunk in range(2):
        counts = []
        for pair in range(2):
            face = chunk * 2 + pair
            column = lax.dot_general(
                eye,
                neighbours[face].astype(F32),
                (((1,), (1,)), ((), ())),
                precision=lax.Precision.HIGHEST,
                preferred_element_type=F32,
            ).astype(jnp.int32)
            entry = [column[:, e : e + 1] for e in range(4)]
            full = entry[3] >= 0
            for e in range(4):
                hot = (lane == entry[e] - first_row) & (entry[e] >= 0)
                rows = pl.ds((pair * 4 + e) * blocks, blocks)
                value = jnp.where(hot & full, 1.0, 0.0).astype(BF16)
                pool_hot[chunk, rows, pl.ds(0, 128)] = value
                pool_hot[chunk, rows, pl.ds(128, 128)] = value
                if e == 0:
                    rows = pl.ds(pair * blocks, blocks)
                    value = jnp.where(hot & jnp.logical_not(full), 1.0, 0.0).astype(BF16)
                    fine_hot[chunk, rows, pl.ds(0, 128)] = value
                    fine_hot[chunk, rows, pl.ds(128, 128)] = value
            counts.append(jnp.where(entry[0] >= 0, 0.5, 0.0))
        present[:, pl.ds(chunk * 128, 128)] = jnp.where(low, counts[0], counts[1])
    low_on = jnp.where(level > 0, 0.5, 0.0)
    high_on = jnp.where(level < layers - 1, 0.5, 0.0)
    present[:, pl.ds(256, 128)] = jnp.where(low, low_on, high_on)
    lift = jnp.where(low, -1.0, 1.0)

    for copy in moves:
        copy.wait()

    meta = got[:, :, pl.ds(4 * CELLS, 128)].reshape(slots, 128)
    spot_got = meta[:, :1]
    flag_got = meta[:, 64:65].astype(jnp.int32)
    shape = (slots, both)
    row = iota(shape, 0)
    used = (
        ((iota(shape, 1) & (blocks - 1)).astype(F32) == spot_got)
        & ((iota(shape, 1) >> shift) == ((row >> 2) & 1))
        & (row >= 8)
    )
    hot = jnp.where(used, 1.0, 0.0).astype(BF16)
    for start in range(0, slots, 16):

        def load(s, j, start=start):
            return got[
                pl.ds(start // 8, 2), :, pl.ds(s * CELLS + j * 128, 128)
            ].reshape(16, 128)

        def store(s, j, value, start=start):
            cols = pl.ds(s * CELLS + j * 128, 128)
            high, rest = split(value)
            got_work[pl.ds(start, 16), cols] = high
            got_work[pl.ds(slots + start, 16), cols] = rest

        adapt_rows(load, store, flag_got[start : start + 16])
    hot = jnp.concatenate([hot, hot], axis=0)
    settled[...] += lax.dot_general(
        hot, got_work[...], (((0,), (0,)), ((), ())), preferred_element_type=F32
    )

    top_rows = pl.ds(0, blocks)
    end_rows = pl.ds(blocks, blocks)
    seg = [pl.ds(s * CELLS, CELLS) for s in range(4)]

    def closure(h):
        n = settled[top_rows, seg[2]]
        m = 1.0 - 1.0 / n
        log_x = jnp.log(settled[top_rows, seg[1]] * jnp.maximum(-h, 0.0))
        log_up = m * jnp.log(1.0 + jnp.exp(n * log_x))
        root = jnp.exp(-0.5 * log_up)
        inner = 1.0 - jnp.exp((n - 1.0) * log_x - log_up)
        resid = settled[end_rows, seg[1]]
        water = resid + (settled[end_rows, seg[2]] - resid) * root * root
        conduct = settled[top_rows, seg[3]] * root * inner * inner
        return water, conduct

    lane_all = iota((blocks, CELLS), 1)

    def evaluate(step, h, diag):
        water, conduct = closure(h)
        terms = jnp.concatenate([*split(h), *split(conduct)], axis=0)
        taken = dot(terms, t_take[...])
        face_h = taken[:blocks] + taken[blocks:both]
        face_k = taken[both : both + blocks] + taken[both + blocks :]
        faces[0] = face_h[:, :256]
        faces[1] = face_k[:, :256]
        edge_h = face_h[:, 256:]
        edge_k = face_k[:, 256:]
        planes[0] = jnp.where(low, edge_h, pltpu.roll(edge_k, 64, 1))
        planes[1] = jnp.where(low, pltpu.roll(edge_h, 64, 1), edge_k)

        def halo_copy(side, way):
            start = 0 if side else blocks - REACH
            return pltpu.make_async_remote_copy(
                src_ref=faces.at[:, pl.ds(start, REACH)],
                dst_ref=halo.at[step, side],
                send_sem=halo_send.at[step, side],
                recv_sem=halo_recv.at[step, side],
                device_id=(me + way, level),
                device_id_type=MESH,
            )

        def plane_copy(side, way):
            return pltpu.make_async_remote_copy(
                src_ref=planes.at[1 - side],
                dst_ref=ghost_planes.at[step, side],
                send_sem=plane_send.at[step, side],
                recv_sem=plane_recv.at[step, side],
                device_id=(me, level + way),
                device_id_type=MESH,
            )

        @pl.when(me < peers - 1)
        def _():
            halo_copy(0, 1).start()

        @pl.when(me > 0)
        def _():
            halo_copy(1, -1).start()

        @pl.when(level < layers - 1)
        def _():
            plane_copy(0, 1).start()

        @pl.when(level > 0)
        def _():
            plane_copy(1, -1).start()

        flux = jnp.zeros((blocks, CELLS), F32)
        total = jnp.zeros((blocks, CELLS), F32)
        for stride, rise in ((64, 0.0), (8, 0.0), (1, 1.0)):
            inside = ((lane_all // stride) & 7) < 7
            near_h = pltpu.roll(h, CELLS - stride, 1)
            near_k = pltpu.roll(conduct, CELLS - stride, 1)
            part = jnp.where(inside, 0.5 * (conduct + near_k), 0.0)
            gain = part * (near_h - h + rise)
            flux = flux + gain - pltpu.roll(gain, stride, 1)
            if diag:
                total = total + part + pltpu.roll(part, stride, 1)
        fields[0] = 4.0 * (water - settled[end_rows, seg[0]]) - flux
        if diag:
            resid = settled[end_rows, seg[1]]
            fields[1] = (
                4.0 * (settled[end_rows, seg[2]] - resid) * settled[top_rows, seg[1]] + total
            )

        @pl.when(me < peers - 1)
        def _():
            halo_copy(0, 1).wait_send()
            halo_copy(1, -1).wait_recv()

        @pl.when(me > 0)
        def _():
            halo_copy(1, -1).wait_send()
            halo_copy(0, 1).wait_recv()

        @pl.when(level < layers - 1)
        def _():
            plane_copy(0, 1).wait_send()
            plane_copy(1, -1).wait_recv()

        @pl.when(level > 0)
        def _():
            plane_copy(1, -1).wait_send()
            plane_copy(0, 1).wait_recv()

        spare = jnp.zeros((128 - blocks - 2 * REACH, 128), F32)
        out_h = []
        out_k = []
        for chunk in range(2):
            cols = pl.ds(chunk * 128, 128)
            terms = []
            for kind in range(2):
                wide = jnp.concatenate(
                    [halo[step, 0, kind, :, cols], faces[kind, :, cols], halo[step, 1, kind, :, cols], spare],
                    axis=0,
                )
                terms.append(jnp.concatenate(split(wide), axis=0))
            pooled = dot(jnp.concatenate(terms, axis=0), t_pool[...])
            pooled = [pooled[:128] + pooled[128:256], pooled[256:384] + pooled[384:]]
            pooled = [jnp.concatenate(split(x), axis=0) for x in pooled]
            fine = dot(fine_hot[chunk], jnp.concatenate(terms, axis=1))
            pool = dot(pool_hot[chunk], jnp.concatenate(pooled, axis=1))
            for kind, out in ((0, out_h), (1, out_k)):
                col = slice(kind * 128, kind * 128 + 128)
                sides = []
                for pair in range(2):
                    quad = [
                        pool[(pair * 4 + e) * blocks : (pair * 4 + e + 1) * blocks, col]
                        for e in range(4)
                    ]
                    hanging = jnp.where(
                        quarter < 2,
                        jnp.where(quarter == 0, quad[0], quad[1]),
                        jnp.where(quarter == 2, quad[2], quad[3]),
                    )
                    sides.append(hanging + fine[pair * blocks : (pair + 1) * blocks, col])
                out.append(pltpu.roll(jnp.where(low, sides[1], sides[0]), 64, 1))
        below = ghost_planes[step, 0]
        above = ghost_planes[step, 1]
        out_h.append(jnp.where(low, below, pltpu.roll(above, 64, 1)) + lift)
        out_k.append(jnp.where(low, pltpu.roll(below, 64, 1), above))
        rim = present[...] * (face_k + jnp.concatenate(out_k, axis=1))
        push = rim * (jnp.concatenate(out_h, axis=1) - face_h)
        if diag:
            spread = dot(jnp.concatenate([*split(push), *split(rim)], axis=0), t_put[...])
            resid = fields[0] - (spread[:blocks] + spread[blocks:both])
            return resid, fields[1] + spread[both : both + blocks] + spread[both + blocks :]
        spread = dot(jnp.concatenate(split(push), axis=0), t_put[...])
        return fields[0] - (spread[:blocks] + spread[blocks:]), None

    start_head = settled[top_rows, seg[0]]
    resid, diag = evaluate(0, start_head, True)
    fresh = start_head - resid / diag
    new_head[0] = fresh
    resid, _ = evaluate(1, fresh, False)
    residual[0] = resid


def on_device(
    peers,
    layers,
    head,
    water_prev,
    alpha,
    shape_n,
    theta_r,
    theta_s,
    sat_cond,
    refine,
    destination,
    neighbours,
):
    blocks = head.shape[1]
    both = 2 * blocks
    slots = 8 * peers
    table = take_table()
    vmem = pl.BlockSpec(memory_space=pltpu.VMEM)
    hbm = pl.BlockSpec(memory_space=pltpu.HBM)
    dma = pltpu.SemaphoreType.DMA
    return pl.pallas_call(
        functools.partial(kernel, peers, layers),
        out_shape=(
            jax.ShapeDtypeStruct(head.shape, F32),
            jax.ShapeDtypeStruct(head.shape, F32),
        ),
        in_specs=[hbm] * 13,
        out_specs=(vmem, vmem),
        scratch_shapes=[pltpu.VMEM(head.shape, F32)] * 7
        + [
            pltpu.VMEM((1, blocks), jnp.int32),
            pltpu.VMEM((1, blocks), jnp.int32),
            pltpu.VMEM((4, 4, blocks), jnp.int32),
            pltpu.VMEM((CELLS, 384), BF16),
            pltpu.VMEM((384, CELLS), BF16),
            pltpu.VMEM((128, 128), BF16),
            dma((13,)),
            pltpu.VMEM((2 * both, 4 * CELLS), BF16),
            pltpu.VMEM((peers, 8, 4 * CELLS + 128), F32),
            pltpu.VMEM((peers, 8, 4 * CELLS + 128), F32),
            pltpu.VMEM((2 * both, 4 * CELLS), BF16),
            pltpu.VMEM((both, 4 * CELLS), F32),
            pltpu.VMEM((2 * slots, 4 * CELLS), BF16),
            pltpu.VMEM((8, 128), F32),
            pltpu.VMEM((2, 2 * blocks, 256), BF16),
            pltpu.VMEM((2, 8 * blocks, 256), BF16),
            pltpu.VMEM((blocks, 384), F32),
            pltpu.VMEM((2, blocks, 256), F32),
            pltpu.VMEM((2, blocks, 128), F32),
            pltpu.VMEM((2, 2, 2, REACH, 256), F32),
            pltpu.VMEM((2, 2, blocks, 128), F32),
            pltpu.VMEM((2, blocks, CELLS), F32),
            dma((peers,)),
            dma((peers,)),
            dma((2, 2)),
            dma((2, 2)),
            dma((2, 2)),
            dma((2, 2)),
        ],
        compiler_params=pltpu.CompilerParams(
            collective_id=0, has_side_effects=True, vmem_limit_bytes=48 * 1024 * 1024
        ),
    )(
        head,
        water_prev,
        alpha,
        shape_n,
        theta_r,
        theta_s,
        sat_cond,
        refine.reshape(1, blocks),
        destination.reshape(1, blocks),
        neighbours.transpose(1, 2, 0),
        jnp.asarray(table, BF16),
        jnp.asarray(table.T, BF16),
        jnp.asarray(pool_table(), BF16),
    )


def solution(mesh):
    cells = P("depth", "dom", None)
    placed = (cells,) * 7 + (P("dom"), P("dom"), P("dom", None, None))
    return jax.shard_map(
        functools.partial(on_device, mesh.shape["dom"], mesh.shape["depth"]),
        mesh=mesh,
        in_specs=placed,
        out_specs=(cells, cells),
        check_vma=False,
    )
```

```python
import functools

import jax
import jax.numpy as jnp
import numpy as np
from jax import lax
from jax.experimental import pallas as pl
from jax.experimental.pallas import tpu as pltpu
from jax.sharding import PartitionSpec as P

MESH = pl.DeviceIdType.MESH
CELLS = 512
CAP = 4
REACH = 16
F32 = jnp.float32
BF16 = jnp.bfloat16


def face_cells(face):
    listed = []
    for first in range(8):
        for second in range(8):
            listed.append(
                (
                    first * 8 + second,
                    448 + first * 8 + second,
                    first * 64 + second,
                    first * 64 + 56 + second,
                    first * 64 + second * 8,
                    first * 64 + second * 8 + 7,
                )[face]
            )
    return listed


def take_table():
    table = np.zeros((CELLS, 384), np.float32)
    for face in range(6):
        for spot, cell in enumerate(face_cells(face)):
            table[cell, face * 64 + spot] = 1.0
    return table


def pool_table():
    table = np.zeros((128, 128), np.float32)
    for half in range(2):
        for a in range(8):
            for b in range(8):
                for u in range(2):
                    for w in range(2):
                        source = (2 * (a % 4) + u) * 8 + 2 * (b % 4) + w
                        table[half * 64 + source, half * 64 + a * 8 + b] = 0.25
    return table


def iota(shape, axis):
    return lax.broadcasted_iota(jnp.int32, shape, axis)


def split(x):
    high = x.astype(BF16)
    return high, (x - high.astype(F32)).astype(BF16)


def dot(a, b):
    return jnp.dot(a, b, preferred_element_type=F32)


def lanes_of(x, index):
    return jnp.take_along_axis(x, index, axis=1, mode="promise_in_bounds")


def adapt_rows(load, store, flags):
    rows = flags.shape[0]
    shape = (rows, 128)
    flag = jnp.broadcast_to(flags, shape)
    octant = jnp.maximum(flag - 1, 0)
    kept = flag == 0
    bx = (octant >> 2) == 1
    by = (octant >> 1) & 1
    bz = octant & 1
    lane = iota(shape, 1)
    y = (lane >> 3) & 7
    z = lane & 7
    half = lane & 64
    low = lane < 64
    ya = 4 * by + (y >> 1)
    za = 4 * bz + (z >> 1)
    yb = jnp.clip(ya + 2 * (y & 1) - 1, 0, 7)
    zb = jnp.clip(za + 2 * (z & 1) - 1, 0, 7)
    index_ya = half + ya * 8 + z
    index_yb = half + yb * 8 + z
    index_za = half + y * 8 + za
    index_zb = half + y * 8 + zb
    index_plain = ya * 8 + za
    v = [load(0, j) for j in range(4)]
    w = [pltpu.roll(chunk, 64, 1) for chunk in v]
    v0 = jnp.where(bx, v[2], v[0])
    v1 = jnp.where(bx, v[3], v[1])
    w0 = jnp.where(bx, w[2], w[0])
    w1 = jnp.where(bx, w[3], w[1])
    before = jnp.where(bx, w[1], v[0])
    after = jnp.where(bx, v[3], w[2])
    near = (
        jnp.where(low, v0, w0),
        jnp.where(low, w0, v0),
        jnp.where(low, v1, w1),
        jnp.where(low, w1, v1),
    )
    far = (
        jnp.where(low, before, v0),
        jnp.where(low, v0, w1),
        jnp.where(low, w0, v1),
        jnp.where(low, v1, after),
    )
    for j in range(4):
        cur = 0.75 * near[j] + 0.25 * far[j]
        cur = 0.75 * lanes_of(cur, index_ya) + 0.25 * lanes_of(cur, index_yb)
        cur = 0.75 * lanes_of(cur, index_za) + 0.25 * lanes_of(cur, index_zb)
        store(0, j, jnp.where(kept, v[j], cur))
    for s in range(1, 4):
        v = [load(s, j) for j in range(4)]
        for j in range(4):
            source = jnp.where(bx, v[2 + j // 2], v[j // 2])
            cur = lanes_of(source, index_plain + (j % 2) * 64)
            store(s, j, jnp.where(kept, v[j], cur))


def kernel(
    peers,
    layers,
    head_hbm,
    water_prev_hbm,
    alpha_hbm,
    shape_n_hbm,
    theta_r_hbm,
    theta_s_hbm,
    sat_cond_hbm,
    refine_hbm,
    destination_hbm,
    neighbours_hbm,
    t_take_hbm,
    t_put_hbm,
    t_pool_hbm,
    new_head,
    residual,
    head,
    water_prev,
    alpha,
    shape_n,
    theta_r,
    theta_s,
    sat_cond,
    refine,
    destination,
    neighbours,
    t_take,
    t_put,
    t_pool,
    load_sem,
    raw,
    sent,
    got,
    work,
    settled,
    got_work,
    place,
    fine_hot,
    pool_hot,
    present,
    faces,
    planes,
    halo,
    ghost_planes,
    fields,
    move_send,
    move_recv,
    halo_send,
    halo_recv,
    plane_send,
    plane_recv,
):
    me = lax.axis_index("dom")
    level = lax.axis_index("depth")
    blocks = head.shape[1]
    both = 2 * blocks
    slots = 8 * peers
    shift = blocks.bit_length() - 1

    loads = []
    for source, target in (
        (destination_hbm, destination),
        (refine_hbm, refine),
        (head_hbm, head),
        (water_prev_hbm, water_prev),
        (alpha_hbm, alpha),
        (theta_r_hbm, theta_r),
        (shape_n_hbm, shape_n),
        (theta_s_hbm, theta_s),
        (sat_cond_hbm, sat_cond),
        (neighbours_hbm, neighbours),
        (t_take_hbm, t_take),
        (t_pool_hbm, t_pool),
        (t_put_hbm, t_put),
    ):
        loads.append(pltpu.make_async_copy(source, target, load_sem.at[len(loads)]))
    for copy in loads:
        copy.start()

    halo[...] = jnp.zeros_like(halo)
    ghost_planes[...] = jnp.zeros_like(ghost_planes)
    got[0] = jnp.zeros(got.shape[1:], F32)

    barrier = pltpu.get_barrier_semaphore()
    for k in range(1, peers):
        pl.semaphore_signal(
            barrier, inc=1, device_id=(lax.rem(me + k, peers), level), device_id_type=MESH
        )

    @pl.when(level > 0)
    def _():
        pl.semaphore_signal(barrier, inc=1, device_id=(me, level - 1), device_id_type=MESH)

    @pl.when(level < layers - 1)
    def _():
        pl.semaphore_signal(barrier, inc=1, device_id=(me, level + 1), device_id_type=MESH)

    for copy in loads[:9]:
        copy.wait()
    left = (head, alpha, shape_n, sat_cond)
    right = (water_prev, theta_r, theta_s)
    for s in range(4):
        cols = pl.ds(s * CELLS, CELLS)
        high, rest = split(left[s][0])
        raw[pl.ds(0, blocks), cols] = high
        raw[pl.ds(both, blocks), cols] = rest
        if s < 3:
            high, rest = split(right[s][0])
            raw[pl.ds(blocks, blocks), cols] = high
            raw[pl.ds(both + blocks, blocks), cols] = rest
        else:
            raw[pl.ds(blocks, blocks), cols] = jnp.zeros((blocks, CELLS), BF16)
            raw[pl.ds(both + blocks, blocks), cols] = jnp.zeros((blocks, CELLS), BF16)

    dest = jnp.concatenate([destination[...], destination[...]], axis=1)
    flag_row = jnp.concatenate([refine[...], refine[...]], axis=1)
    owner = dest >> shift
    spot = dest & (blocks - 1)
    shape = (blocks, both)
    own_lane = iota(shape, 1)
    own_row = iota(shape, 0)
    diagonal = own_lane == own_row
    owner_col = jnp.sum(jnp.where(diagonal, owner, 0), axis=1, keepdims=True)
    flag_col = jnp.sum(jnp.where(diagonal, flag_row, 0), axis=1, keepdims=True)
    earlier = (owner_col == owner) & (own_row < (own_lane & (blocks - 1)))
    rank = jnp.sum(earlier.astype(jnp.int32), axis=0, keepdims=True)
    shape = (slots, both)
    row = iota(shape, 0)
    side = (row >> 2) & 1
    target = me + (row >> 3)
    target = jnp.where(target >= peers, target - peers, target)
    chosen = (
        (side == (iota(shape, 1) >> shift))
        & (owner == target)
        & (rank == (row & 3))
        & (row >= 8)
    )
    hot = jnp.where(chosen, 1.0, 0.0)
    spot_sent = jnp.sum(hot * (spot + 1).astype(F32), axis=1, keepdims=True) - 1.0
    flag_sent = jnp.sum(hot * flag_row.astype(F32), axis=1, keepdims=True)
    hot = hot.astype(BF16)
    packed = dot(jnp.concatenate([hot, hot], axis=1), raw[...])
    sent[:, :, pl.ds(0, 4 * CELLS)] = packed.reshape(peers, 8, 4 * CELLS)
    meta = jnp.where(iota((slots, 128), 1) < 64, spot_sent, flag_sent)
    sent[:, :, pl.ds(4 * CELLS, 128)] = meta.reshape(peers, 8, 128)

    @pl.when((level > 0) & (level < layers - 1))
    def _():
        pl.semaphore_wait(barrier, peers + 1)

    @pl.when((level == 0) | (level == layers - 1))
    def _():
        pl.semaphore_wait(barrier, peers)

    moves = []
    for k in range(1, peers):
        moves.append(
            pltpu.make_async_remote_copy(
                src_ref=sent.at[k],
                dst_ref=got.at[k],
                send_sem=move_send.at[k],
                recv_sem=move_recv.at[k],
                device_id=(lax.rem(me + k, peers), level),
                device_id_type=MESH,
            )
        )
    for copy in moves:
        copy.start()

    flags16 = flag_col
    for start in range(0, both, 16):
        base = start % blocks

        def load(s, j, start=start, base=base):
            refs = left if start < blocks else right
            if s == 3 and start >= blocks:
                return jnp.zeros((16, 128), F32)
            return refs[s][0, pl.ds(base, 16), pl.ds(j * 128, 128)]

        def store(s, j, value, start=start):
            cols = pl.ds(s * CELLS + j * 128, 128)
            high, rest = split(value)
            work[pl.ds(start, 16), cols] = high
            work[pl.ds(both + start, 16), cols] = rest

        adapt_rows(load, store, flags16[base : base + 16])
    shape = (both, both)
    wanted = (
        (iota(shape, 0) - spot == ((iota(shape, 0) >> shift) << shift))
        & ((iota(shape, 0) >> shift) == (iota(shape, 1) >> shift))
        & (owner == me)
    )
    hot = jnp.where(wanted, 1.0, 0.0).astype(BF16)
    settled[...] = dot(jnp.concatenate([hot, hot], axis=1), work[...])

    for copy in loads[9:]:
        copy.wait()
    first_row = me * blocks - REACH
    eye = jnp.where(iota((blocks, blocks), 0) == iota((blocks, blocks), 1), 1.0, 0.0)
    shape = (blocks, 128)
    lane = iota(shape, 1)
    low = lane < 64
    quarter = ((lane >> 5) & 1) * 2 + ((lane >> 2) & 1)
    for chunk in range(2):
        counts = []
        for pair in range(2):
            face = chunk * 2 + pair
            column = lax.dot_general(
                eye,
                neighbours[face].astype(F32),
                (((1,), (1,)), ((), ())),
                precision=lax.Precision.HIGHEST,
                preferred_element_type=F32,
            ).astype(jnp.int32)
            entry = [column[:, e : e + 1] for e in range(4)]
            full = entry[3] >= 0
            for e in range(4):
                hot = (lane == entry[e] - first_row) & (entry[e] >= 0)
                rows = pl.ds((pair * 4 + e) * blocks, blocks)
                value = jnp.where(hot & full, 1.0, 0.0).astype(BF16)
                pool_hot[chunk, rows, pl.ds(0, 128)] = value
                pool_hot[chunk, rows, pl.ds(128, 128)] = value
                if e == 0:
                    rows = pl.ds(pair * blocks, blocks)
                    value = jnp.where(hot & jnp.logical_not(full), 1.0, 0.0).astype(BF16)
                    fine_hot[chunk, rows, pl.ds(0, 128)] = value
                    fine_hot[chunk, rows, pl.ds(128, 128)] = value
            counts.append(jnp.where(entry[0] >= 0, 0.5, 0.0))
        present[:, pl.ds(chunk * 128, 128)] = jnp.where(low, counts[0], counts[1])
    low_on = jnp.where(level > 0, 0.5, 0.0)
    high_on = jnp.where(level < layers - 1, 0.5, 0.0)
    present[:, pl.ds(256, 128)] = jnp.where(low, low_on, high_on)
    lift = jnp.where(low, -1.0, 1.0)

    for copy in moves:
        copy.wait()

    meta = got[:, :, pl.ds(4 * CELLS, 128)].reshape(slots, 128)
    spot_got = meta[:, :1]
    flag_got = meta[:, 64:65].astype(jnp.int32)
    shape = (slots, both)
    row = iota(shape, 0)
    used = (
        ((iota(shape, 1) & (blocks - 1)).astype(F32) == spot_got)
        & ((iota(shape, 1) >> shift) == ((row >> 2) & 1))
        & (row >= 8)
    )
    hot = jnp.where(used, 1.0, 0.0).astype(BF16)
    for start in range(0, slots, 16):

        def load(s, j, start=start):
            return got[
                pl.ds(start // 8, 2), :, pl.ds(s * CELLS + j * 128, 128)
            ].reshape(16, 128)

        def store(s, j, value, start=start):
            cols = pl.ds(s * CELLS + j * 128, 128)
            high, rest = split(value)
            got_work[pl.ds(start, 16), cols] = high
            got_work[pl.ds(slots + start, 16), cols] = rest

        adapt_rows(load, store, flag_got[start : start + 16])
    hot = jnp.concatenate([hot, hot], axis=0)
    settled[...] += lax.dot_general(
        hot, got_work[...], (((0,), (0,)), ((), ())), preferred_element_type=F32
    )

    top_rows = pl.ds(0, blocks)
    end_rows = pl.ds(blocks, blocks)
    seg = [pl.ds(s * CELLS, CELLS) for s in range(4)]

    def closure(h):
        n = settled[top_rows, seg[2]]
        m = 1.0 - 1.0 / n
        log_x = jnp.log(settled[top_rows, seg[1]] * jnp.maximum(-h, 0.0))
        log_up = m * jnp.log(1.0 + jnp.exp(n * log_x))
        root = jnp.exp(-0.5 * log_up)
        inner = 1.0 - jnp.exp((n - 1.0) * log_x - log_up)
        resid = settled[end_rows, seg[1]]
        water = resid + (settled[end_rows, seg[2]] - resid) * root * root
        conduct = settled[top_rows, seg[3]] * root * inner * inner
        return water, conduct

    lane_all = iota((blocks, CELLS), 1)

    def evaluate(step, h, diag):
        water, conduct = closure(h)
        terms = jnp.concatenate([*split(h), *split(conduct)], axis=0)
        taken = dot(terms, t_take[...])
        face_h = taken[:blocks] + taken[blocks:both]
        face_k = taken[both : both + blocks] + taken[both + blocks :]
        faces[0] = face_h[:, :256]
        faces[1] = face_k[:, :256]
        edge_h = face_h[:, 256:]
        edge_k = face_k[:, 256:]
        planes[0] = jnp.where(low, edge_h, pltpu.roll(edge_k, 64, 1))
        planes[1] = jnp.where(low, pltpu.roll(edge_h, 64, 1), edge_k)

        def halo_copy(side, way):
            start = 0 if side else blocks - REACH
            return pltpu.make_async_remote_copy(
                src_ref=faces.at[:, pl.ds(start, REACH)],
                dst_ref=halo.at[step, side],
                send_sem=halo_send.at[step, side],
                recv_sem=halo_recv.at[step, side],
                device_id=(me + way, level),
                device_id_type=MESH,
            )

        def plane_copy(side, way):
            return pltpu.make_async_remote_copy(
                src_ref=planes.at[1 - side],
                dst_ref=ghost_planes.at[step, side],
                send_sem=plane_send.at[step, side],
                recv_sem=plane_recv.at[step, side],
                device_id=(me, level + way),
                device_id_type=MESH,
            )

        @pl.when(me < peers - 1)
        def _():
            halo_copy(0, 1).start()

        @pl.when(me > 0)
        def _():
            halo_copy(1, -1).start()

        @pl.when(level < layers - 1)
        def _():
            plane_copy(0, 1).start()

        @pl.when(level > 0)
        def _():
            plane_copy(1, -1).start()

        flux = jnp.zeros((blocks, CELLS), F32)
        total = jnp.zeros((blocks, CELLS), F32)
        for stride, rise in ((64, 0.0), (8, 0.0), (1, 1.0)):
            inside = ((lane_all // stride) & 7) < 7
            near_h = pltpu.roll(h, CELLS - stride, 1)
            near_k = pltpu.roll(conduct, CELLS - stride, 1)
            part = jnp.where(inside, 0.5 * (conduct + near_k), 0.0)
            gain = part * (near_h - h + rise)
            flux = flux + gain - pltpu.roll(gain, stride, 1)
            if diag:
                total = total + part + pltpu.roll(part, stride, 1)
        fields[0] = 4.0 * (water - settled[end_rows, seg[0]]) - flux
        if diag:
            resid = settled[end_rows, seg[1]]
            fields[1] = (
                4.0 * (settled[end_rows, seg[2]] - resid) * settled[top_rows, seg[1]] + total
            )

        @pl.when(me < peers - 1)
        def _():
            halo_copy(0, 1).wait_send()
            halo_copy(1, -1).wait_recv()

        @pl.when(me > 0)
        def _():
            halo_copy(1, -1).wait_send()
            halo_copy(0, 1).wait_recv()

        @pl.when(level < layers - 1)
        def _():
            plane_copy(0, 1).wait_send()
            plane_copy(1, -1).wait_recv()

        @pl.when(level > 0)
        def _():
            plane_copy(1, -1).wait_send()
            plane_copy(0, 1).wait_recv()

        spare = jnp.zeros((128 - blocks - 2 * REACH, 128), F32)
        out_h = []
        out_k = []
        for chunk in range(2):
            cols = pl.ds(chunk * 128, 128)
            terms = []
            for kind in range(2):
                wide = jnp.concatenate(
                    [halo[step, 0, kind, :, cols], faces[kind, :, cols], halo[step, 1, kind, :, cols], spare],
                    axis=0,
                )
                terms.append(jnp.concatenate(split(wide), axis=0))
            pooled = dot(jnp.concatenate(terms, axis=0), t_pool[...])
            pooled = [pooled[:128] + pooled[128:256], pooled[256:384] + pooled[384:]]
            pooled = [jnp.concatenate(split(x), axis=0) for x in pooled]
            fine = dot(fine_hot[chunk], jnp.concatenate(terms, axis=1))
            pool = dot(pool_hot[chunk], jnp.concatenate(pooled, axis=1))
            for kind, out in ((0, out_h), (1, out_k)):
                col = slice(kind * 128, kind * 128 + 128)
                sides = []
                for pair in range(2):
                    quad = [
                        pool[(pair * 4 + e) * blocks : (pair * 4 + e + 1) * blocks, col]
                        for e in range(4)
                    ]
                    hanging = jnp.where(
                        quarter < 2,
                        jnp.where(quarter == 0, quad[0], quad[1]),
                        jnp.where(quarter == 2, quad[2], quad[3]),
                    )
                    sides.append(hanging + fine[pair * blocks : (pair + 1) * blocks, col])
                out.append(pltpu.roll(jnp.where(low, sides[1], sides[0]), 64, 1))
        below = ghost_planes[step, 0]
        above = ghost_planes[step, 1]
        out_h.append(jnp.where(low, below, pltpu.roll(above, 64, 1)) + lift)
        out_k.append(jnp.where(low, pltpu.roll(below, 64, 1), above))
        rim = present[...] * (face_k + jnp.concatenate(out_k, axis=1))
        push = rim * (jnp.concatenate(out_h, axis=1) - face_h)
        if diag:
            spread = dot(jnp.concatenate([*split(push), *split(rim)], axis=0), t_put[...])
            resid = fields[0] - (spread[:blocks] + spread[blocks:both])
            return resid, fields[1] + spread[both : both + blocks] + spread[both + blocks :]
        spread = dot(jnp.concatenate(split(push), axis=0), t_put[...])
        return fields[0] - (spread[:blocks] + spread[blocks:]), None

    start_head = settled[top_rows, seg[0]]
    resid, diag = evaluate(0, start_head, True)
    fresh = start_head - resid / diag
    new_head[0] = fresh
    resid, _ = evaluate(1, fresh, False)
    residual[0] = resid


def on_device(
    peers,
    layers,
    head,
    water_prev,
    alpha,
    shape_n,
    theta_r,
    theta_s,
    sat_cond,
    refine,
    destination,
    neighbours,
):
    blocks = head.shape[1]
    both = 2 * blocks
    slots = 8 * peers
    table = take_table()
    vmem = pl.BlockSpec(memory_space=pltpu.VMEM)
    hbm = pl.BlockSpec(memory_space=pltpu.HBM)
    dma = pltpu.SemaphoreType.DMA
    return pl.pallas_call(
        functools.partial(kernel, peers, layers),
        out_shape=(
            jax.ShapeDtypeStruct(head.shape, F32),
            jax.ShapeDtypeStruct(head.shape, F32),
        ),
        in_specs=[hbm] * 13,
        out_specs=(vmem, vmem),
        scratch_shapes=[pltpu.VMEM(head.shape, F32)] * 7
        + [
            pltpu.VMEM((1, blocks), jnp.int32),
            pltpu.VMEM((1, blocks), jnp.int32),
            pltpu.VMEM((4, 4, blocks), jnp.int32),
            pltpu.VMEM((CELLS, 384), BF16),
            pltpu.VMEM((384, CELLS), BF16),
            pltpu.VMEM((128, 128), BF16),
            dma((13,)),
            pltpu.VMEM((2 * both, 4 * CELLS), BF16),
            pltpu.VMEM((peers, 8, 4 * CELLS + 128), F32),
            pltpu.VMEM((peers, 8, 4 * CELLS + 128), F32),
            pltpu.VMEM((2 * both, 4 * CELLS), BF16),
            pltpu.VMEM((both, 4 * CELLS), F32),
            pltpu.VMEM((2 * slots, 4 * CELLS), BF16),
            pltpu.VMEM((8, 128), F32),
            pltpu.VMEM((2, 2 * blocks, 256), BF16),
            pltpu.VMEM((2, 8 * blocks, 256), BF16),
            pltpu.VMEM((blocks, 384), F32),
            pltpu.VMEM((2, blocks, 256), F32),
            pltpu.VMEM((2, blocks, 128), F32),
            pltpu.VMEM((2, 2, 2, REACH, 256), F32),
            pltpu.VMEM((2, 2, blocks, 128), F32),
            pltpu.VMEM((2, blocks, CELLS), F32),
            dma((peers,)),
            dma((peers,)),
            dma((2, 2)),
            dma((2, 2)),
            dma((2, 2)),
            dma((2, 2)),
        ],
        compiler_params=pltpu.CompilerParams(
            collective_id=0, has_side_effects=True, vmem_limit_bytes=60 * 1024 * 1024
        ),
    )(
        head,
        water_prev,
        alpha,
        shape_n,
        theta_r,
        theta_s,
        sat_cond,
        refine.reshape(1, blocks),
        destination.reshape(1, blocks),
        neighbours.transpose(1, 2, 0),
        jnp.asarray(table, BF16),
        jnp.asarray(table.T, BF16),
        jnp.asarray(pool_table(), BF16),
    )


def solution(mesh):
    cells = P("depth", "dom", None)
    placed = (cells,) * 7 + (P("dom"), P("dom"), P("dom", None, None))
    return jax.shard_map(
        functools.partial(on_device, mesh.shape["dom"], mesh.shape["depth"]),
        mesh=mesh,
        in_specs=placed,
        out_specs=(cells, cells),
        check_vma=False,
    )
```

```python
import functools

import jax
import jax.numpy as jnp
import numpy as np
from jax import lax
from jax.experimental import pallas as pl
from jax.experimental.pallas import tpu as pltpu
from jax.sharding import PartitionSpec as P

MESH = pl.DeviceIdType.MESH
CELLS = 512
CAP = 4
REACH = 16
F32 = jnp.float32
BF16 = jnp.bfloat16


def face_cells(face):
    listed = []
    for first in range(8):
        for second in range(8):
            listed.append(
                (
                    first * 8 + second,
                    448 + first * 8 + second,
                    first * 64 + second,
                    first * 64 + 56 + second,
                    first * 64 + second * 8,
                    first * 64 + second * 8 + 7,
                )[face]
            )
    return listed


def take_table():
    table = np.zeros((CELLS, 384), np.float32)
    for face in range(6):
        for spot, cell in enumerate(face_cells(face)):
            table[cell, face * 64 + spot] = 1.0
    return table


def pool_table():
    table = np.zeros((128, 128), np.float32)
    for half in range(2):
        for a in range(8):
            for b in range(8):
                for u in range(2):
                    for w in range(2):
                        source = (2 * (a % 4) + u) * 8 + 2 * (b % 4) + w
                        table[half * 64 + source, half * 64 + a * 8 + b] = 0.25
    return table


def iota(shape, axis):
    return lax.broadcasted_iota(jnp.int32, shape, axis)


def split(x):
    high = x.astype(BF16)
    return high, (x - high.astype(F32)).astype(BF16)


def dot(a, b):
    return jnp.dot(a, b, preferred_element_type=F32)


def lanes_of(x, index):
    return jnp.take_along_axis(x, index, axis=1, mode="promise_in_bounds")


def adapt_rows(load, flags, plain):
    made = {}

    def store(s, j, value):
        made[s, j] = value

    rows = flags.shape[0]
    shape = (rows, 128)
    flag = jnp.broadcast_to(flags, shape)
    octant = jnp.maximum(flag - 1, 0)
    kept = flag == 0
    bx = (octant >> 2) == 1
    by = (octant >> 1) & 1
    bz = octant & 1
    lane = iota(shape, 1)
    y = (lane >> 3) & 7
    z = lane & 7
    half = lane & 64
    low = lane < 64
    ya = 4 * by + (y >> 1)
    za = 4 * bz + (z >> 1)
    yb = jnp.clip(ya + 2 * (y & 1) - 1, 0, 7)
    zb = jnp.clip(za + 2 * (z & 1) - 1, 0, 7)
    index_ya = half + ya * 8 + z
    index_yb = half + yb * 8 + z
    index_za = half + y * 8 + za
    index_zb = half + y * 8 + zb
    index_plain = ya * 8 + za
    v = [load(0, j) for j in range(4)]
    w = [pltpu.roll(chunk, 64, 1) for chunk in v]
    v0 = jnp.where(bx, v[2], v[0])
    v1 = jnp.where(bx, v[3], v[1])
    w0 = jnp.where(bx, w[2], w[0])
    w1 = jnp.where(bx, w[3], w[1])
    before = jnp.where(bx, w[1], v[0])
    after = jnp.where(bx, v[3], w[2])
    near = (
        jnp.where(low, v0, w0),
        jnp.where(low, w0, v0),
        jnp.where(low, v1, w1),
        jnp.where(low, w1, v1),
    )
    far = (
        jnp.where(low, before, v0),
        jnp.where(low, v0, w1),
        jnp.where(low, w0, v1),
        jnp.where(low, v1, after),
    )
    for j in range(4):
        cur = 0.75 * near[j] + 0.25 * far[j]
        cur = 0.75 * lanes_of(cur, index_ya) + 0.25 * lanes_of(cur, index_yb)
        cur = 0.75 * lanes_of(cur, index_za) + 0.25 * lanes_of(cur, index_zb)
        store(0, j, jnp.where(kept, v[j], cur))
    for s in range(1, plain + 1):
        v = [load(s, j) for j in range(4)]
        for j in range(4):
            source = jnp.where(bx, v[2 + j // 2], v[j // 2])
            cur = lanes_of(source, index_plain + (j % 2) * 64)
            store(s, j, jnp.where(kept, v[j], cur))
    return made


def closure(h, alpha, n, cond):
    m = 1.0 - 1.0 / n
    log_x = jnp.log(alpha * jnp.maximum(-h, 0.0))
    log_up = m * jnp.log(1.0 + jnp.exp(n * log_x))
    root = jnp.exp(-0.5 * log_up)
    if cond is None:
        return root, None
    inner = 1.0 - jnp.exp((n - 1.0) * log_x - log_up)
    return root, cond * root * inner * inner


def kernel(
    peers,
    layers,
    head_hbm,
    water_prev_hbm,
    alpha_hbm,
    shape_n_hbm,
    theta_r_hbm,
    theta_s_hbm,
    sat_cond_hbm,
    refine_hbm,
    destination_hbm,
    neighbours_hbm,
    t_take_hbm,
    t_put_hbm,
    t_pool_hbm,
    new_head,
    residual,
    head,
    water_prev,
    alpha,
    shape_n,
    theta_r,
    theta_s,
    sat_cond,
    refine,
    destination,
    neighbours,
    t_take,
    t_put,
    t_pool,
    load_sem,
    raw,
    sent_a,
    sent_b,
    got_a,
    got_b,
    work_a,
    work_b,
    place,
    settled_a,
    settled_b,
    own_hot,
    halo_hot,
    present,
    faces,
    ghosts,
    halo,
    ghost_planes,
    a_send,
    a_recv,
    b_send,
    b_recv,
    halo_send,
    halo_recv,
    plane_send,
    plane_recv,
):
    me = lax.axis_index("dom")
    level = lax.axis_index("depth")
    blocks = head.shape[1]
    both = 2 * blocks
    slots = 8 * peers
    shift = blocks.bit_length() - 1

    loads = []
    for source, target in (
        (destination_hbm, destination),
        (refine_hbm, refine),
        (head_hbm, head),
        (water_prev_hbm, water_prev),
        (alpha_hbm, alpha),
        (theta_r_hbm, theta_r),
        (shape_n_hbm, shape_n),
        (theta_s_hbm, theta_s),
        (sat_cond_hbm, sat_cond),
        (neighbours_hbm, neighbours),
        (t_take_hbm, t_take),
        (t_pool_hbm, t_pool),
        (t_put_hbm, t_put),
    ):
        loads.append(pltpu.make_async_copy(source, target, load_sem.at[len(loads)]))
    for copy in loads:
        copy.start()

    halo[...] = jnp.zeros_like(halo)
    ghost_planes[...] = jnp.zeros_like(ghost_planes)
    got_a[0] = jnp.zeros(got_a.shape[1:], F32)
    got_b[0] = jnp.zeros(got_b.shape[1:], F32)

    barrier = pltpu.get_barrier_semaphore()
    for k in range(1, peers):
        pl.semaphore_signal(
            barrier, inc=1, device_id=(lax.rem(me + k, peers), level), device_id_type=MESH
        )

    @pl.when(level > 0)
    def _():
        pl.semaphore_signal(barrier, inc=1, device_id=(me, level - 1), device_id_type=MESH)

    @pl.when(level < layers - 1)
    def _():
        pl.semaphore_signal(barrier, inc=1, device_id=(me, level + 1), device_id_type=MESH)

    for copy in loads[:9]:
        copy.wait()
    left = (head, alpha, shape_n, sat_cond)
    right = (water_prev, theta_r, theta_s)
    for s in range(4):
        cols = pl.ds(s * CELLS, CELLS)
        high, rest = split(left[s][0])
        raw[pl.ds(0, blocks), cols] = high
        raw[pl.ds(both, blocks), cols] = rest
        if s < 3:
            high, rest = split(right[s][0])
            raw[pl.ds(blocks, blocks), cols] = high
            raw[pl.ds(both + blocks, blocks), cols] = rest
        else:
            raw[pl.ds(blocks, blocks), cols] = jnp.zeros((blocks, CELLS), BF16)
            raw[pl.ds(both + blocks, blocks), cols] = jnp.zeros((blocks, CELLS), BF16)

    dest = jnp.concatenate([destination[...], destination[...]], axis=1)
    flag_row = jnp.concatenate([refine[...], refine[...]], axis=1)
    owner = dest >> shift
    spot = dest & (blocks - 1)
    shape = (blocks, both)
    own_lane = iota(shape, 1)
    own_row = iota(shape, 0)
    diagonal = own_lane == own_row
    owner_col = jnp.sum(jnp.where(diagonal, owner, 0), axis=1, keepdims=True)
    flag_col = jnp.sum(jnp.where(diagonal, flag_row, 0), axis=1, keepdims=True)
    earlier = (owner_col == owner) & (own_row < (own_lane & (blocks - 1)))
    rank = jnp.sum(earlier.astype(jnp.int32), axis=0, keepdims=True)
    shape = (slots, both)
    row = iota(shape, 0)
    side = (row >> 2) & 1
    target = me + (row >> 3)
    target = jnp.where(target >= peers, target - peers, target)
    chosen = (
        (side == (iota(shape, 1) >> shift))
        & (owner == target)
        & (rank == (row & 3))
        & (row >= 8)
    )
    hot = jnp.where(chosen, 1.0, 0.0)
    spot_sent = jnp.sum(hot * (spot + 1).astype(F32), axis=1, keepdims=True) - 1.0
    flag_sent = jnp.sum(hot * flag_row.astype(F32), axis=1, keepdims=True)
    hot = hot.astype(BF16)
    packed = dot(jnp.concatenate([hot, hot], axis=1), raw[...])
    filled = spot_sent >= 0.0
    for start in range(0, slots, 16):
        rows = slice(start, start + 16)
        made = adapt_rows(
            lambda s, j: packed[rows, s * CELLS + j * 128 : s * CELLS + (j + 1) * 128],
            flag_sent[rows].astype(jnp.int32),
            3,
        )
        upper = (iota((16, 128), 0) & 4) == 0
        peer = pl.ds(start // 8, 2)
        for j in range(4):
            conduct = closure(made[0, j], made[1, j], made[2, j], made[3, j])[1]
            conduct = jnp.where(filled[rows], conduct, 0.0)
            pair = jnp.where(upper, made[0, j], pltpu.roll(conduct, 4, 0))
            sent_a[peer, :, pl.ds(j * 128, 128)] = pair.reshape(2, 8, 128)
            for s, value in (
                (0, made[1, j]),
                (1, made[2, j]),
                (2, jnp.where(upper, made[3, j], made[0, j])),
            ):
                cols = pl.ds(s * CELLS + j * 128, 128)
                sent_b[peer, :, cols] = value.reshape(2, 8, 128)
        meta = jnp.broadcast_to(spot_sent[rows], (16, 128))
        sent_a[peer, :, pl.ds(CELLS, 128)] = meta.reshape(2, 8, 128)

    @pl.when((level > 0) & (level < layers - 1))
    def _():
        pl.semaphore_wait(barrier, peers + 1)

    @pl.when((level == 0) | (level == layers - 1))
    def _():
        pl.semaphore_wait(barrier, peers)

    moves_a = []
    moves_b = []
    for moves, source, target, gone, come in (
        (moves_a, sent_a, got_a, a_send, a_recv),
        (moves_b, sent_b, got_b, b_send, b_recv),
    ):
        for k in range(1, peers):
            moves.append(
                pltpu.make_async_remote_copy(
                    src_ref=source.at[k],
                    dst_ref=target.at[k],
                    send_sem=gone.at[k],
                    recv_sem=come.at[k],
                    device_id=(lax.rem(me + k, peers), level),
                    device_id_type=MESH,
                )
            )
    for copy in moves_a + moves_b:
        copy.start()

    def put_rows(work, start, cols, value):
        high, rest = split(value)
        work[pl.ds(start, 16), cols] = high
        work[pl.ds(both + start, 16), cols] = rest

    for start in range(0, blocks, 16):
        made = adapt_rows(
            lambda s, j: left[s][0, pl.ds(start, 16), pl.ds(j * 128, 128)],
            flag_col[start : start + 16],
            3,
        )
        for j in range(4):
            conduct = closure(made[0, j], made[1, j], made[2, j], made[3, j])[1]
            put_rows(work_a, start, pl.ds(j * 128, 128), made[0, j])
            put_rows(work_a, blocks + start, pl.ds(j * 128, 128), conduct)
            for s in range(3):
                put_rows(work_b, start, pl.ds(s * CELLS + j * 128, 128), made[s + 1, j])
    shape = (both, both)
    wanted = (
        ((iota(shape, 0) & (blocks - 1)) == spot)
        & ((iota(shape, 0) >> shift) == (iota(shape, 1) >> shift))
        & (owner == me)
    )
    hot = jnp.where(wanted, 1.0, 0.0).astype(BF16)
    place[...] = jnp.concatenate([hot, hot], axis=1)
    settled_a[...] = dot(place[...], work_a[...])

    for copy in loads[9:]:
        copy.wait()
    eye = jnp.where(iota((blocks, blocks), 0) == iota((blocks, blocks), 1), 1.0, 0.0)
    shape = (blocks, 128)
    lane = iota(shape, 1)
    low = lane < 64
    for face in range(4):
        column = lax.dot_general(
            eye,
            neighbours[face].astype(F32),
            (((1,), (1,)), ((), ())),
            precision=lax.Precision.HIGHEST,
            preferred_element_type=F32,
        ).astype(jnp.int32)
        entry = [jnp.broadcast_to(column[:, e : e + 1], shape) for e in range(4)]
        full = entry[3] >= 0
        present[face] = jnp.where(entry[0] >= 0, 0.5, 0.0)
        wants = [jnp.where(full, -1, entry[0])] + [jnp.where(full, entry[e], -1) for e in range(4)]
        outer = []
        for number, want in enumerate(wants):
            gap = want - me * blocks
            listed = want >= 0
            hit = ((lane & (blocks - 1)) == gap) & listed
            own_hot[face, :, pl.ds(number * 128, 128)] = jnp.where(hit, 1.0, 0.0).astype(BF16)
            spot_out = jnp.where(gap < 0, gap + REACH, gap - blocks + REACH)
            hit = ((lane & (2 * REACH - 1)) == spot_out) & listed & ((gap < 0) | (gap >= blocks))
            outer.append(jnp.where(hit, 1.0, 0.0))
        outer.append(jnp.zeros(shape, F32))
        for number in range(3):
            value = jnp.where(low, outer[2 * number], outer[2 * number + 1])
            halo_hot[face, :, pl.ds(number * 128, 128)] = value.astype(BF16)
    low_on = jnp.where(level > 0, 0.5, 0.0)
    high_on = jnp.where(level < layers - 1, 0.5, 0.0)
    lane_q = iota((128, 128), 1)
    quarter = ((lane_q >> 5) & 1) * 2 + ((lane_q >> 2) & 1)
    masks = [jnp.where(quarter == e, 1.0, 0.0).astype(BF16) for e in range(4)]

    for copy in moves_a:
        copy.wait_recv()
    spot_got = got_a[:, :, pl.ds(CELLS, 128)].reshape(slots, 128)
    shape = (slots, both)
    row = iota(shape, 0)
    used = (
        ((iota(shape, 1) & (blocks - 1)).astype(F32) == spot_got)
        & ((iota(shape, 1) >> shift) == ((row >> 2) & 1))
        & (row >= 8)
    )
    hot = jnp.where(used, 1.0, 0.0).astype(BF16)
    used_hot = jnp.concatenate([hot, hot], axis=0)

    def scatter(value):
        return lax.dot_general(
            used_hot,
            jnp.concatenate(split(value), axis=0),
            (((0,), (0,)), ((), ())),
            preferred_element_type=F32,
        )

    settled_a[...] += scatter(got_a[:, :, pl.ds(0, CELLS)].reshape(slots, CELLS))

    top_rows = pl.ds(0, blocks)
    end_rows = pl.ds(blocks, blocks)
    seg = [pl.ds(s * CELLS, CELLS) for s in range(3)]
    lane_all = iota((blocks, CELLS), 1)

    def other_fields():
        for start in range(0, blocks, 16):
            made = adapt_rows(
                lambda s, j: right[s][0, pl.ds(start, 16), pl.ds(j * 128, 128)],
                flag_col[start : start + 16],
                2,
            )
            for j in range(4):
                for s, value in ((0, made[1, j]), (1, made[2, j]), (2, made[0, j])):
                    put_rows(work_b, blocks + start, pl.ds(s * CELLS + j * 128, 128), value)
        settled_b[...] = dot(place[...], work_b[...])
        for copy in moves_b:
            copy.wait_recv()
        settled_b[...] += scatter(got_b[...].reshape(slots, 3 * CELLS))

    def water_of(root):
        resid = settled_b[end_rows, seg[0]]
        return resid + (settled_b[end_rows, seg[1]] - resid) * root * root

    def gather_table(high, rest, pooled_high, pooled_rest):
        parts = [high, rest]
        for mask in masks:
            parts += [pooled_high * mask[: high.shape[0]], pooled_rest * mask[: high.shape[0]]]
        return parts

    def pool(stacked):
        high, rest = split(stacked)
        both_parts = dot(jnp.concatenate([high, rest], axis=0), t_pool[...])
        count = stacked.shape[0]
        pooled_high, pooled_rest = split(both_parts[:count] + both_parts[count:])
        return high, rest, pooled_high, pooled_rest

    opposite = (1, 0, 3, 2)

    def evaluate(step, h, conduct, meanwhile):
        terms = jnp.concatenate([*split(h), *split(conduct)], axis=0)
        taken = dot(terms, t_take[...])
        face_h = taken[:blocks] + taken[blocks:both]
        face_k = taken[both : both + blocks] + taken[both + blocks :]
        for chunk in range(3):
            part_h = face_h[:, chunk * 128 : chunk * 128 + 128]
            part_k = face_k[:, chunk * 128 : chunk * 128 + 128]
            faces[2 * chunk] = jnp.where(low, part_h, pltpu.roll(part_k, 64, 1))
            faces[2 * chunk + 1] = jnp.where(low, pltpu.roll(part_h, 64, 1), part_k)

        def halo_copy(side, way):
            start = 0 if side else blocks - REACH
            return pltpu.make_async_remote_copy(
                src_ref=faces.at[pl.ds(0, 4), pl.ds(start, REACH)],
                dst_ref=halo.at[step, side],
                send_sem=halo_send.at[step, side],
                recv_sem=halo_recv.at[step, side],
                device_id=(me + way, level),
                device_id_type=MESH,
            )

        def plane_copy(side, way):
            return pltpu.make_async_remote_copy(
                src_ref=faces.at[5 - side],
                dst_ref=ghost_planes.at[step, side],
                send_sem=plane_send.at[step, side],
                recv_sem=plane_recv.at[step, side],
                device_id=(me, level + way),
                device_id_type=MESH,
            )

        @pl.when(me < peers - 1)
        def _():
            halo_copy(0, 1).start()

        @pl.when(me > 0)
        def _():
            halo_copy(1, -1).start()

        @pl.when(level < layers - 1)
        def _():
            plane_copy(0, 1).start()

        @pl.when(level > 0)
        def _():
            plane_copy(1, -1).start()

        flux = jnp.zeros((blocks, CELLS), F32)
        total = jnp.zeros((blocks, CELLS), F32)
        for stride, rise in ((64, 0.0), (8, 0.0), (1, 1.0)):
            inside = (lane_all & (7 * stride)) < 7 * stride
            near_h = pltpu.roll(h, CELLS - stride, 1)
            near_k = pltpu.roll(conduct, CELLS - stride, 1)
            part = jnp.where(inside, 0.5 * (conduct + near_k), 0.0)
            gain = part * (near_h - h + rise)
            flux = flux + gain - pltpu.roll(gain, stride, 1)
            if step == 0:
                total = total + part + pltpu.roll(part, stride, 1)
        parts = pool(faces[pl.ds(0, 4)].reshape(4 * blocks, 128))
        for face in range(4):
            rows = slice(opposite[face] * blocks, (opposite[face] + 1) * blocks)
            table = gather_table(*[part[rows] for part in parts])
            ghosts[face] = dot(own_hot[face], jnp.concatenate(table, axis=0))
        resid, diag = meanwhile(flux, total)

        @pl.when(me < peers - 1)
        def _():
            halo_copy(0, 1).wait_send()
            halo_copy(1, -1).wait_recv()

        @pl.when(me > 0)
        def _():
            halo_copy(1, -1).wait_send()
            halo_copy(0, 1).wait_recv()

        @pl.when(level < layers - 1)
        def _():
            plane_copy(0, 1).wait_send()
            plane_copy(1, -1).wait_recv()

        @pl.when(level > 0)
        def _():
            plane_copy(1, -1).wait_send()
            plane_copy(0, 1).wait_recv()

        wide = 2 * REACH
        stacked = [halo[step, side, face] for face in range(4) for side in range(2)]
        parts = pool(jnp.concatenate(stacked, axis=0))
        spare = jnp.zeros((2 * wide, 128), BF16)
        sums = []
        gaps = []
        for face in range(4):
            rows = slice(opposite[face] * wide, (opposite[face] + 1) * wide)
            table = gather_table(*[part[rows] for part in parts]) + [spare]
            ghost = ghosts[face] + dot(halo_hot[face], jnp.concatenate(table, axis=0))
            sums.append(present[face] * (faces[face] + ghost))
            gaps.append(ghost - faces[face])
        for side, on, lift in ((0, low_on, -1.0), (1, high_on, 1.0)):
            ghost = ghost_planes[step, side]
            sums.append(on * (faces[4 + side] + ghost))
            gaps.append(ghost - faces[4 + side] + lift)
        push = []
        rim = []
        for first in range(0, 6, 2):
            here = pltpu.roll(sums[first], 64, 1)
            there = sums[first + 1]
            push.append(
                jnp.where(low, here * gaps[first], there * pltpu.roll(gaps[first + 1], 64, 1))
            )
            rim.append(jnp.where(low, here, there))
        push = jnp.concatenate(push, axis=1)
        rim = jnp.concatenate(rim, axis=1)
        if step == 0:
            spread = dot(jnp.concatenate([*split(push), *split(rim)], axis=0), t_put[...])
            diag = diag + spread[both : both + blocks] + spread[both + blocks :]
        else:
            spread = dot(jnp.concatenate(split(push), axis=0), t_put[...])
        return resid - (spread[:blocks] + spread[blocks:both]), diag

    start_head = settled_a[top_rows]

    def first_balance(flux, total):
        other_fields()
        alpha_here = settled_b[top_rows, seg[0]]
        n = settled_b[top_rows, seg[1]]
        root = closure(start_head, alpha_here, n, None)[0]
        resid = 4.0 * (water_of(root) - settled_b[end_rows, seg[2]]) - flux
        room = settled_b[end_rows, seg[1]] - settled_b[end_rows, seg[0]]
        return resid, 4.0 * room * alpha_here + total

    resid, diag = evaluate(0, start_head, settled_a[end_rows], first_balance)
    fresh = start_head - resid / diag
    new_head[0] = fresh
    root, conduct = closure(
        fresh, settled_b[top_rows, seg[0]], settled_b[top_rows, seg[1]], settled_b[top_rows, seg[2]]
    )

    def second_balance(flux, total):
        return 4.0 * (water_of(root) - settled_b[end_rows, seg[2]]) - flux, None

    residual[0] = evaluate(1, fresh, conduct, second_balance)[0]
    for copy in moves_a + moves_b:
        copy.wait_send()


def on_device(
    peers,
    layers,
    head,
    water_prev,
    alpha,
    shape_n,
    theta_r,
    theta_s,
    sat_cond,
    refine,
    destination,
    neighbours,
):
    blocks = head.shape[1]
    both = 2 * blocks
    slots = 8 * peers
    table = take_table()
    vmem = pl.BlockSpec(memory_space=pltpu.VMEM)
    hbm = pl.BlockSpec(memory_space=pltpu.HBM)
    dma = pltpu.SemaphoreType.DMA
    return pl.pallas_call(
        functools.partial(kernel, peers, layers),
        out_shape=(
            jax.ShapeDtypeStruct(head.shape, F32),
            jax.ShapeDtypeStruct(head.shape, F32),
        ),
        in_specs=[hbm] * 13,
        out_specs=(vmem, vmem),
        scratch_shapes=[pltpu.VMEM(head.shape, F32)] * 7
        + [
            pltpu.VMEM((1, blocks), jnp.int32),
            pltpu.VMEM((1, blocks), jnp.int32),
            pltpu.VMEM((4, 4, blocks), jnp.int32),
            pltpu.VMEM((CELLS, 384), BF16),
            pltpu.VMEM((384, CELLS), BF16),
            pltpu.VMEM((128, 128), BF16),
            dma((13,)),
            pltpu.VMEM((2 * both, 4 * CELLS), BF16),
            pltpu.VMEM((peers, 8, CELLS + 128), F32),
            pltpu.VMEM((peers, 8, 3 * CELLS), F32),
            pltpu.VMEM((peers, 8, CELLS + 128), F32),
            pltpu.VMEM((peers, 8, 3 * CELLS), F32),
            pltpu.VMEM((2 * both, CELLS), BF16),
            pltpu.VMEM((2 * both, 3 * CELLS), BF16),
            pltpu.VMEM((both, 2 * both), BF16),
            pltpu.VMEM((both, CELLS), F32),
            pltpu.VMEM((both, 3 * CELLS), F32),
            pltpu.VMEM((4, blocks, 640), BF16),
            pltpu.VMEM((4, blocks, 384), BF16),
            pltpu.VMEM((4, blocks, 128), F32),
            pltpu.VMEM((6, blocks, 128), F32),
            pltpu.VMEM((4, blocks, 128), F32),
            pltpu.VMEM((2, 2, 4, REACH, 128), F32),
            pltpu.VMEM((2, 2, blocks, 128), F32),
            dma((peers,)),
            dma((peers,)),
            dma((peers,)),
            dma((peers,)),
            dma((2, 2)),
            dma((2, 2)),
            dma((2, 2)),
            dma((2, 2)),
        ],
        compiler_params=pltpu.CompilerParams(
            collective_id=0, has_side_effects=True, vmem_limit_bytes=60 * 1024 * 1024
        ),
    )(
        head,
        water_prev,
        alpha,
        shape_n,
        theta_r,
        theta_s,
        sat_cond,
        refine.reshape(1, blocks),
        destination.reshape(1, blocks),
        neighbours.transpose(1, 2, 0),
        jnp.asarray(table, BF16),
        jnp.asarray(table.T, BF16),
        jnp.asarray(pool_table(), BF16),
    )


def solution(mesh):
    cells = P("depth", "dom", None)
    placed = (cells,) * 7 + (P("dom"), P("dom"), P("dom", None, None))
    return jax.shard_map(
        functools.partial(on_device, mesh.shape["dom"], mesh.shape["depth"]),
        mesh=mesh,
        in_specs=placed,
        out_specs=(cells, cells),
        check_vma=False,
    )
```

```python
import functools

import jax
import jax.numpy as jnp
import numpy as np
from jax import lax
from jax.experimental import pallas as pl
from jax.experimental.pallas import tpu as pltpu
from jax.sharding import PartitionSpec as P

MESH = pl.DeviceIdType.MESH
CELLS = 512
CAP = 4
REACH = 16
F32 = jnp.float32
BF16 = jnp.bfloat16


def face_cells(face):
    listed = []
    for first in range(8):
        for second in range(8):
            listed.append(
                (
                    first * 8 + second,
                    448 + first * 8 + second,
                    first * 64 + second,
                    first * 64 + 56 + second,
                    first * 64 + second * 8,
                    first * 64 + second * 8 + 7,
                )[face]
            )
    return listed


def take_table():
    table = np.zeros((CELLS, 384), np.float32)
    for face in range(6):
        for spot, cell in enumerate(face_cells(face)):
            table[cell, face * 64 + spot] = 1.0
    return table


def pool_table():
    table = np.zeros((128, 128), np.float32)
    for half in range(2):
        for a in range(8):
            for b in range(8):
                for u in range(2):
                    for w in range(2):
                        source = (2 * (a % 4) + u) * 8 + 2 * (b % 4) + w
                        table[half * 64 + source, half * 64 + a * 8 + b] = 0.25
    return table


def iota(shape, axis):
    return lax.broadcasted_iota(jnp.int32, shape, axis)


def split(x):
    high = x.astype(BF16)
    return high, (x - high.astype(F32)).astype(BF16)


def dot(a, b):
    return jnp.dot(a, b, preferred_element_type=F32)


def lanes_of(x, index):
    return jnp.take_along_axis(x, index, axis=1, mode="promise_in_bounds")


def adapt_rows(load, flags, plain):
    made = {}

    def store(s, j, value):
        made[s, j] = value

    rows = flags.shape[0]
    shape = (rows, 128)
    flag = jnp.broadcast_to(flags, shape)
    octant = jnp.maximum(flag - 1, 0)
    kept = flag == 0
    bx = (octant >> 2) == 1
    by = (octant >> 1) & 1
    bz = octant & 1
    lane = iota(shape, 1)
    y = (lane >> 3) & 7
    z = lane & 7
    half = lane & 64
    low = lane < 64
    ya = 4 * by + (y >> 1)
    za = 4 * bz + (z >> 1)
    yb = jnp.clip(ya + 2 * (y & 1) - 1, 0, 7)
    zb = jnp.clip(za + 2 * (z & 1) - 1, 0, 7)
    index_ya = half + ya * 8 + z
    index_yb = half + yb * 8 + z
    index_za = half + y * 8 + za
    index_zb = half + y * 8 + zb
    index_plain = ya * 8 + za
    v = [load(0, j) for j in range(4)]
    w = [pltpu.roll(chunk, 64, 1) for chunk in v]
    v0 = jnp.where(bx, v[2], v[0])
    v1 = jnp.where(bx, v[3], v[1])
    w0 = jnp.where(bx, w[2], w[0])
    w1 = jnp.where(bx, w[3], w[1])
    before = jnp.where(bx, w[1], v[0])
    after = jnp.where(bx, v[3], w[2])
    near = (
        jnp.where(low, v0, w0),
        jnp.where(low, w0, v0),
        jnp.where(low, v1, w1),
        jnp.where(low, w1, v1),
    )
    far = (
        jnp.where(low, before, v0),
        jnp.where(low, v0, w1),
        jnp.where(low, w0, v1),
        jnp.where(low, v1, after),
    )
    for j in range(4):
        cur = 0.75 * near[j] + 0.25 * far[j]
        cur = 0.75 * lanes_of(cur, index_ya) + 0.25 * lanes_of(cur, index_yb)
        cur = 0.75 * lanes_of(cur, index_za) + 0.25 * lanes_of(cur, index_zb)
        store(0, j, jnp.where(kept, v[j], cur))
    for s in range(1, plain + 1):
        v = [load(s, j) for j in range(4)]
        for j in range(4):
            source = jnp.where(bx, v[2 + j // 2], v[j // 2])
            cur = lanes_of(source, index_plain + (j % 2) * 64)
            store(s, j, jnp.where(kept, v[j], cur))
    return made


def closure(h, alpha, n, cond):
    m = 1.0 - 1.0 / n
    log_x = jnp.log(alpha * jnp.maximum(-h, 0.0))
    log_up = m * jnp.log(1.0 + jnp.exp(n * log_x))
    root = jnp.exp(-0.5 * log_up)
    if cond is None:
        return root, None
    inner = 1.0 - jnp.exp((n - 1.0) * log_x - log_up)
    return root, cond * root * inner * inner


def kernel(
    peers,
    layers,
    head_hbm,
    water_prev_hbm,
    alpha_hbm,
    shape_n_hbm,
    theta_r_hbm,
    theta_s_hbm,
    sat_cond_hbm,
    refine_hbm,
    destination_hbm,
    neighbours_hbm,
    t_take_hbm,
    t_put_hbm,
    t_pool_hbm,
    new_head,
    residual,
    head,
    water_prev,
    alpha,
    shape_n,
    theta_r,
    theta_s,
    sat_cond,
    refine,
    destination,
    neighbours,
    t_take,
    t_put,
    t_pool,
    load_sem,
    raw,
    sent_a,
    sent_b,
    got_a,
    got_b,
    work_a,
    work_b,
    place,
    settled_a,
    settled_b,
    own_hot,
    halo_hot,
    present,
    faces,
    ghosts,
    halo,
    ghost_planes,
    a_send,
    a_recv,
    b_send,
    b_recv,
    halo_send,
    halo_recv,
    plane_send,
    plane_recv,
):
    me = lax.axis_index("dom")
    level = lax.axis_index("depth")
    blocks = head.shape[1]
    both = 2 * blocks
    slots = 8 * peers
    shift = blocks.bit_length() - 1

    loads = []
    for source, target in (
        (destination_hbm, destination),
        (refine_hbm, refine),
        (head_hbm, head),
        (water_prev_hbm, water_prev),
        (alpha_hbm, alpha),
        (theta_r_hbm, theta_r),
        (shape_n_hbm, shape_n),
        (theta_s_hbm, theta_s),
        (sat_cond_hbm, sat_cond),
        (neighbours_hbm, neighbours),
        (t_take_hbm, t_take),
        (t_pool_hbm, t_pool),
        (t_put_hbm, t_put),
    ):
        loads.append(pltpu.make_async_copy(source, target, load_sem.at[len(loads)]))
    for copy in loads:
        copy.start()

    halo[...] = jnp.zeros_like(halo)
    ghost_planes[...] = jnp.zeros_like(ghost_planes)
    got_a[0] = jnp.zeros(got_a.shape[1:], F32)
    got_b[0] = jnp.zeros(got_b.shape[1:], F32)

    barrier = pltpu.get_barrier_semaphore()
    for k in range(1, peers):
        pl.semaphore_signal(
            barrier, inc=1, device_id=(lax.rem(me + k, peers), level), device_id_type=MESH
        )

    @pl.when(level > 0)
    def _():
        pl.semaphore_signal(barrier, inc=1, device_id=(me, level - 1), device_id_type=MESH)

    @pl.when(level < layers - 1)
    def _():
        pl.semaphore_signal(barrier, inc=1, device_id=(me, level + 1), device_id_type=MESH)

    for copy in loads[:9]:
        copy.wait()
    left = (head, alpha, shape_n, sat_cond)
    right = (water_prev, theta_r, theta_s)
    for s in range(4):
        cols = pl.ds(s * CELLS, CELLS)
        high, rest = split(left[s][0])
        raw[pl.ds(0, blocks), cols] = high
        raw[pl.ds(both, blocks), cols] = rest
        if s < 3:
            high, rest = split(right[s][0])
            raw[pl.ds(blocks, blocks), cols] = high
            raw[pl.ds(both + blocks, blocks), cols] = rest
        else:
            raw[pl.ds(blocks, blocks), cols] = jnp.zeros((blocks, CELLS), BF16)
            raw[pl.ds(both + blocks, blocks), cols] = jnp.zeros((blocks, CELLS), BF16)

    dest = jnp.concatenate([destination[...], destination[...]], axis=1)
    flag_row = jnp.concatenate([refine[...], refine[...]], axis=1)
    owner = dest >> shift
    spot = dest & (blocks - 1)
    shape = (blocks, both)
    own_lane = iota(shape, 1)
    own_row = iota(shape, 0)
    diagonal = own_lane == own_row
    owner_col = jnp.sum(jnp.where(diagonal, owner, 0), axis=1, keepdims=True)
    flag_col = jnp.sum(jnp.where(diagonal, flag_row, 0), axis=1, keepdims=True)
    earlier = (owner_col == owner) & (own_row < (own_lane & (blocks - 1)))
    rank = jnp.sum(earlier.astype(jnp.int32), axis=0, keepdims=True)
    shape = (slots, both)
    row = iota(shape, 0)
    side = (row >> 2) & 1
    target = me + (row >> 3)
    target = jnp.where(target >= peers, target - peers, target)
    chosen = (
        (side == (iota(shape, 1) >> shift))
        & (owner == target)
        & (rank == (row & 3))
        & (row >= 8)
    )
    hot = jnp.where(chosen, 1.0, 0.0)
    spot_sent = jnp.sum(hot * (spot + 1).astype(F32), axis=1, keepdims=True) - 1.0
    flag_sent = jnp.sum(hot * flag_row.astype(F32), axis=1, keepdims=True)
    hot = hot.astype(BF16)
    packed = dot(jnp.concatenate([hot, hot], axis=1), raw[...])
    filled = spot_sent >= 0.0
    for start in range(0, slots, 16):
        rows = slice(start, start + 16)
        made = adapt_rows(
            lambda s, j: packed[rows, s * CELLS + j * 128 : s * CELLS + (j + 1) * 128],
            flag_sent[rows].astype(jnp.int32),
            3,
        )
        upper = (iota((16, 128), 0) & 4) == 0
        peer = pl.ds(start // 8, 2)
        for j in range(4):
            conduct = closure(made[0, j], made[1, j], made[2, j], made[3, j])[1]
            conduct = jnp.where(filled[rows], conduct, 0.0)
            pair = jnp.where(upper, made[0, j], pltpu.roll(conduct, 4, 0))
            sent_a[peer, :, pl.ds(j * 128, 128)] = pair.reshape(2, 8, 128)
            for s, value in (
                (0, made[1, j]),
                (1, made[2, j]),
                (2, jnp.where(upper, made[3, j], made[0, j])),
            ):
                cols = pl.ds(s * CELLS + j * 128, 128)
                sent_b[peer, :, cols] = value.reshape(2, 8, 128)
        meta = jnp.broadcast_to(spot_sent[rows], (16, 128))
        sent_a[peer, :, pl.ds(CELLS, 128)] = meta.reshape(2, 8, 128)

    @pl.when((level > 0) & (level < layers - 1))
    def _():
        pl.semaphore_wait(barrier, peers + 1)

    @pl.when((level == 0) | (level == layers - 1))
    def _():
        pl.semaphore_wait(barrier, peers)

    moves_a = []
    moves_b = []
    for moves, source, target, gone, come in (
        (moves_a, sent_a, got_a, a_send, a_recv),
        (moves_b, sent_b, got_b, b_send, b_recv),
    ):
        for k in range(1, peers):
            moves.append(
                pltpu.make_async_remote_copy(
                    src_ref=source.at[k],
                    dst_ref=target.at[k],
                    send_sem=gone.at[k],
                    recv_sem=come.at[k],
                    device_id=(lax.rem(me + k, peers), level),
                    device_id_type=MESH,
                )
            )
    for copy in moves_a:
        copy.start()

    def put_rows(work, start, cols, value):
        high, rest = split(value)
        work[pl.ds(start, 16), cols] = high
        work[pl.ds(both + start, 16), cols] = rest

    for start in range(0, blocks, 16):
        made = adapt_rows(
            lambda s, j: left[s][0, pl.ds(start, 16), pl.ds(j * 128, 128)],
            flag_col[start : start + 16],
            3,
        )
        for j in range(4):
            conduct = closure(made[0, j], made[1, j], made[2, j], made[3, j])[1]
            put_rows(work_a, start, pl.ds(j * 128, 128), made[0, j])
            put_rows(work_a, blocks + start, pl.ds(j * 128, 128), conduct)
            for s in range(3):
                put_rows(work_b, start, pl.ds(s * CELLS + j * 128, 128), made[s + 1, j])
    shape = (both, both)
    wanted = (
        ((iota(shape, 0) & (blocks - 1)) == spot)
        & ((iota(shape, 0) >> shift) == (iota(shape, 1) >> shift))
        & (owner == me)
    )
    hot = jnp.where(wanted, 1.0, 0.0).astype(BF16)
    place[...] = jnp.concatenate([hot, hot], axis=1)
    settled_a[...] = dot(place[...], work_a[...])
    for copy in moves_b:
        copy.start()

    for copy in loads[9:]:
        copy.wait()
    eye = jnp.where(iota((blocks, blocks), 0) == iota((blocks, blocks), 1), 1.0, 0.0)
    shape = (blocks, 128)
    lane = iota(shape, 1)
    low = lane < 64
    for face in range(4):
        column = lax.dot_general(
            eye,
            neighbours[face].astype(F32),
            (((1,), (1,)), ((), ())),
            precision=lax.Precision.HIGHEST,
            preferred_element_type=F32,
        ).astype(jnp.int32)
        entry = [jnp.broadcast_to(column[:, e : e + 1], shape) for e in range(4)]
        full = entry[3] >= 0
        present[face] = jnp.where(entry[0] >= 0, 0.5, 0.0)
        wants = [jnp.where(full, -1, entry[0])] + [jnp.where(full, entry[e], -1) for e in range(4)]
        outer = []
        for number, want in enumerate(wants):
            gap = want - me * blocks
            listed = want >= 0
            hit = ((lane & (blocks - 1)) == gap) & listed
            own_hot[face, :, pl.ds(number * 128, 128)] = jnp.where(hit, 1.0, 0.0).astype(BF16)
            spot_out = jnp.where(gap < 0, gap + REACH, gap - blocks + REACH)
            hit = ((lane & (2 * REACH - 1)) == spot_out) & listed & ((gap < 0) | (gap >= blocks))
            outer.append(jnp.where(hit, 1.0, 0.0))
        outer.append(jnp.zeros(shape, F32))
        for number in range(3):
            value = jnp.where(low, outer[2 * number], outer[2 * number + 1])
            halo_hot[face, :, pl.ds(number * 128, 128)] = value.astype(BF16)
    low_on = jnp.where(level > 0, 0.5, 0.0)
    high_on = jnp.where(level < layers - 1, 0.5, 0.0)
    lane_q = iota((128, 128), 1)
    quarter = ((lane_q >> 5) & 1) * 2 + ((lane_q >> 2) & 1)
    masks = [jnp.where(quarter == e, 1.0, 0.0).astype(BF16) for e in range(4)]

    for copy in moves_a:
        copy.wait_recv()
    spot_got = got_a[:, :, pl.ds(CELLS, 128)].reshape(slots, 128)
    shape = (slots, both)
    row = iota(shape, 0)
    used = (
        ((iota(shape, 1) & (blocks - 1)).astype(F32) == spot_got)
        & ((iota(shape, 1) >> shift) == ((row >> 2) & 1))
        & (row >= 8)
    )
    hot = jnp.where(used, 1.0, 0.0).astype(BF16)
    used_hot = jnp.concatenate([hot, hot], axis=0)

    def scatter(value):
        return lax.dot_general(
            used_hot,
            jnp.concatenate(split(value), axis=0),
            (((0,), (0,)), ((), ())),
            preferred_element_type=F32,
        )

    settled_a[...] += scatter(got_a[:, :, pl.ds(0, CELLS)].reshape(slots, CELLS))

    top_rows = pl.ds(0, blocks)
    end_rows = pl.ds(blocks, blocks)
    seg = [pl.ds(s * CELLS, CELLS) for s in range(3)]
    lane_all = iota((blocks, CELLS), 1)

    def other_fields():
        for start in range(0, blocks, 16):
            made = adapt_rows(
                lambda s, j: right[s][0, pl.ds(start, 16), pl.ds(j * 128, 128)],
                flag_col[start : start + 16],
                2,
            )
            for j in range(4):
                for s, value in ((0, made[1, j]), (1, made[2, j]), (2, made[0, j])):
                    put_rows(work_b, blocks + start, pl.ds(s * CELLS + j * 128, 128), value)
        settled_b[...] = dot(place[...], work_b[...])
        for copy in moves_b:
            copy.wait_recv()
        settled_b[...] += scatter(got_b[...].reshape(slots, 3 * CELLS))

    def water_of(root):
        resid = settled_b[end_rows, seg[0]]
        return resid + (settled_b[end_rows, seg[1]] - resid) * root * root

    def gather_table(high, rest, pooled_high, pooled_rest):
        parts = [high, rest]
        for mask in masks:
            parts += [pooled_high * mask[: high.shape[0]], pooled_rest * mask[: high.shape[0]]]
        return parts

    def pool(stacked):
        high, rest = split(stacked)
        both_parts = dot(jnp.concatenate([high, rest], axis=0), t_pool[...])
        count = stacked.shape[0]
        pooled_high, pooled_rest = split(both_parts[:count] + both_parts[count:])
        return high, rest, pooled_high, pooled_rest

    opposite = (1, 0, 3, 2)

    def evaluate(step, h, conduct, meanwhile):
        terms = jnp.concatenate([*split(h), *split(conduct)], axis=0)
        taken = dot(terms, t_take[...])
        face_h = taken[:blocks] + taken[blocks:both]
        face_k = taken[both : both + blocks] + taken[both + blocks :]
        for chunk in range(3):
            part_h = face_h[:, chunk * 128 : chunk * 128 + 128]
            part_k = face_k[:, chunk * 128 : chunk * 128 + 128]
            faces[2 * chunk] = jnp.where(low, part_h, pltpu.roll(part_k, 64, 1))
            faces[2 * chunk + 1] = jnp.where(low, pltpu.roll(part_h, 64, 1), part_k)

        def halo_copy(side, way):
            start = 0 if side else blocks - REACH
            return pltpu.make_async_remote_copy(
                src_ref=faces.at[pl.ds(0, 4), pl.ds(start, REACH)],
                dst_ref=halo.at[step, side],
                send_sem=halo_send.at[step, side],
                recv_sem=halo_recv.at[step, side],
                device_id=(me + way, level),
                device_id_type=MESH,
            )

        def plane_copy(side, way):
            return pltpu.make_async_remote_copy(
                src_ref=faces.at[5 - side],
                dst_ref=ghost_planes.at[step, side],
                send_sem=plane_send.at[step, side],
                recv_sem=plane_recv.at[step, side],
                device_id=(me, level + way),
                device_id_type=MESH,
            )

        @pl.when(me < peers - 1)
        def _():
            halo_copy(0, 1).start()

        @pl.when(me > 0)
        def _():
            halo_copy(1, -1).start()

        @pl.when(level < layers - 1)
        def _():
            plane_copy(0, 1).start()

        @pl.when(level > 0)
        def _():
            plane_copy(1, -1).start()

        flux = jnp.zeros((blocks, CELLS), F32)
        total = jnp.zeros((blocks, CELLS), F32)
        for stride, rise in ((64, 0.0), (8, 0.0), (1, 1.0)):
            inside = (lane_all & (7 * stride)) < 7 * stride
            near_h = pltpu.roll(h, CELLS - stride, 1)
            near_k = pltpu.roll(conduct, CELLS - stride, 1)
            part = jnp.where(inside, 0.5 * (conduct + near_k), 0.0)
            gain = part * (near_h - h + rise)
            flux = flux + gain - pltpu.roll(gain, stride, 1)
            if step == 0:
                total = total + part + pltpu.roll(part, stride, 1)
        parts = pool(faces[pl.ds(0, 4)].reshape(4 * blocks, 128))
        for face in range(4):
            rows = slice(opposite[face] * blocks, (opposite[face] + 1) * blocks)
            table = gather_table(*[part[rows] for part in parts])
            ghosts[face] = dot(own_hot[face], jnp.concatenate(table, axis=0))
        resid, diag = meanwhile(flux, total)

        @pl.when(me < peers - 1)
        def _():
            halo_copy(0, 1).wait_send()
            halo_copy(1, -1).wait_recv()

        @pl.when(me > 0)
        def _():
            halo_copy(1, -1).wait_send()
            halo_copy(0, 1).wait_recv()

        @pl.when(level < layers - 1)
        def _():
            plane_copy(0, 1).wait_send()
            plane_copy(1, -1).wait_recv()

        @pl.when(level > 0)
        def _():
            plane_copy(1, -1).wait_send()
            plane_copy(0, 1).wait_recv()

        wide = 2 * REACH
        stacked = [halo[step, side, face] for face in range(4) for side in range(2)]
        parts = pool(jnp.concatenate(stacked, axis=0))
        spare = jnp.zeros((2 * wide, 128), BF16)
        sums = []
        gaps = []
        for face in range(4):
            rows = slice(opposite[face] * wide, (opposite[face] + 1) * wide)
            table = gather_table(*[part[rows] for part in parts]) + [spare]
            ghost = ghosts[face] + dot(halo_hot[face], jnp.concatenate(table, axis=0))
            sums.append(present[face] * (faces[face] + ghost))
            gaps.append(ghost - faces[face])
        for side, on, lift in ((0, low_on, -1.0), (1, high_on, 1.0)):
            ghost = ghost_planes[step, side]
            sums.append(on * (faces[4 + side] + ghost))
            gaps.append(ghost - faces[4 + side] + lift)
        push = []
        rim = []
        for first in range(0, 6, 2):
            here = pltpu.roll(sums[first], 64, 1)
            there = sums[first + 1]
            push.append(
                jnp.where(low, here * gaps[first], there * pltpu.roll(gaps[first + 1], 64, 1))
            )
            rim.append(jnp.where(low, here, there))
        push = jnp.concatenate(push, axis=1)
        rim = jnp.concatenate(rim, axis=1)
        if step == 0:
            spread = dot(jnp.concatenate([*split(push), *split(rim)], axis=0), t_put[...])
            diag = diag + spread[both : both + blocks] + spread[both + blocks :]
        else:
            spread = dot(jnp.concatenate(split(push), axis=0), t_put[...])
        return resid - (spread[:blocks] + spread[blocks:both]), diag

    start_head = settled_a[top_rows]

    def first_balance(flux, total):
        other_fields()
        alpha_here = settled_b[top_rows, seg[0]]
        n = settled_b[top_rows, seg[1]]
        root = closure(start_head, alpha_here, n, None)[0]
        resid = 4.0 * (water_of(root) - settled_b[end_rows, seg[2]]) - flux
        room = settled_b[end_rows, seg[1]] - settled_b[end_rows, seg[0]]
        return resid, 4.0 * room * alpha_here + total

    resid, diag = evaluate(0, start_head, settled_a[end_rows], first_balance)
    fresh = start_head - resid / diag
    new_head[0] = fresh
    root, conduct = closure(
        fresh, settled_b[top_rows, seg[0]], settled_b[top_rows, seg[1]], settled_b[top_rows, seg[2]]
    )

    def second_balance(flux, total):
        return 4.0 * (water_of(root) - settled_b[end_rows, seg[2]]) - flux, None

    residual[0] = evaluate(1, fresh, conduct, second_balance)[0]
    for copy in moves_a + moves_b:
        copy.wait_send()


def hand_over(first, second, first_out, second_out, sem):
    copies = [
        pltpu.make_async_copy(first, first_out, sem.at[0]),
        pltpu.make_async_copy(second, second_out, sem.at[1]),
    ]
    for copy in copies:
        copy.start()
    for copy in copies:
        copy.wait()


def on_device(
    peers,
    layers,
    head,
    water_prev,
    alpha,
    shape_n,
    theta_r,
    theta_s,
    sat_cond,
    refine,
    destination,
    neighbours,
):
    blocks = head.shape[1]
    both = 2 * blocks
    slots = 8 * peers
    table = take_table()
    vmem = pl.BlockSpec(memory_space=pltpu.VMEM)
    hbm = pl.BlockSpec(memory_space=pltpu.HBM)
    dma = pltpu.SemaphoreType.DMA
    out_shape = (
        jax.ShapeDtypeStruct(head.shape, F32),
        jax.ShapeDtypeStruct(head.shape, F32),
    )
    results = pl.pallas_call(
        functools.partial(kernel, peers, layers),
        out_shape=out_shape,
        in_specs=[hbm] * 13,
        out_specs=(vmem, vmem),
        scratch_shapes=[pltpu.VMEM(head.shape, F32)] * 7
        + [
            pltpu.VMEM((1, blocks), jnp.int32),
            pltpu.VMEM((1, blocks), jnp.int32),
            pltpu.VMEM((4, 4, blocks), jnp.int32),
            pltpu.VMEM((CELLS, 384), BF16),
            pltpu.VMEM((384, CELLS), BF16),
            pltpu.VMEM((128, 128), BF16),
            dma((13,)),
            pltpu.VMEM((2 * both, 4 * CELLS), BF16),
            pltpu.VMEM((peers, 8, CELLS + 128), F32),
            pltpu.VMEM((peers, 8, 3 * CELLS), F32),
            pltpu.VMEM((peers, 8, CELLS + 128), F32),
            pltpu.VMEM((peers, 8, 3 * CELLS), F32),
            pltpu.VMEM((2 * both, CELLS), BF16),
            pltpu.VMEM((2 * both, 3 * CELLS), BF16),
            pltpu.VMEM((both, 2 * both), BF16),
            pltpu.VMEM((both, CELLS), F32),
            pltpu.VMEM((both, 3 * CELLS), F32),
            pltpu.VMEM((4, blocks, 640), BF16),
            pltpu.VMEM((4, blocks, 384), BF16),
            pltpu.VMEM((4, blocks, 128), F32),
            pltpu.VMEM((6, blocks, 128), F32),
            pltpu.VMEM((4, blocks, 128), F32),
            pltpu.VMEM((2, 2, 4, REACH, 128), F32),
            pltpu.VMEM((2, 2, blocks, 128), F32),
            dma((peers,)),
            dma((peers,)),
            dma((peers,)),
            dma((peers,)),
            dma((2, 2)),
            dma((2, 2)),
            dma((2, 2)),
            dma((2, 2)),
        ],
        compiler_params=pltpu.CompilerParams(
            collective_id=0, has_side_effects=True, vmem_limit_bytes=60 * 1024 * 1024
        ),
    )(
        head,
        water_prev,
        alpha,
        shape_n,
        theta_r,
        theta_s,
        sat_cond,
        refine.reshape(1, blocks),
        destination.reshape(1, blocks),
        neighbours.transpose(1, 2, 0),
        jnp.asarray(table, BF16),
        jnp.asarray(table.T, BF16),
        jnp.asarray(pool_table(), BF16),
    )
    return pl.pallas_call(
        hand_over,
        out_shape=out_shape,
        in_specs=[hbm, hbm],
        out_specs=(hbm, hbm),
        scratch_shapes=[dma((2,))],
        compiler_params=pltpu.CompilerParams(vmem_limit_bytes=60 * 1024 * 1024),
    )(*results)


def solution(mesh):
    cells = P("depth", "dom", None)
    placed = (cells,) * 7 + (P("dom"), P("dom"), P("dom", None, None))
    return jax.shard_map(
        functools.partial(on_device, mesh.shape["dom"], mesh.shape["depth"]),
        mesh=mesh,
        in_specs=placed,
        out_specs=(cells, cells),
        check_vma=False,
    )
```

```python
import functools

import jax
import jax.numpy as jnp
import numpy as np
from jax import lax
from jax.experimental import pallas as pl
from jax.experimental.pallas import tpu as pltpu
from jax.sharding import PartitionSpec as P

MESH = pl.DeviceIdType.MESH
CELLS = 512
CAP = 4
REACH = 16
F32 = jnp.float32
BF16 = jnp.bfloat16


def face_cells(face):
    listed = []
    for first in range(8):
        for second in range(8):
            listed.append(
                (
                    first * 8 + second,
                    448 + first * 8 + second,
                    first * 64 + second,
                    first * 64 + 56 + second,
                    first * 64 + second * 8,
                    first * 64 + second * 8 + 7,
                )[face]
            )
    return listed


def take_table():
    table = np.zeros((CELLS, 384), np.float32)
    for face in range(6):
        for spot, cell in enumerate(face_cells(face)):
            table[cell, face * 64 + spot] = 1.0
    return table


def pool_table():
    table = np.zeros((128, 128), np.float32)
    for half in range(2):
        for a in range(8):
            for b in range(8):
                for u in range(2):
                    for w in range(2):
                        source = (2 * (a % 4) + u) * 8 + 2 * (b % 4) + w
                        table[half * 64 + source, half * 64 + a * 8 + b] = 0.25
    return table


def iota(shape, axis):
    return lax.broadcasted_iota(jnp.int32, shape, axis)


def split(x):
    high = x.astype(BF16)
    return high, (x - high.astype(F32)).astype(BF16)


def dot(a, b):
    return jnp.dot(a, b, preferred_element_type=F32)


def lanes_of(x, index):
    return jnp.take_along_axis(x, index, axis=1, mode="promise_in_bounds")


def adapt_rows(load, flags, plain):
    made = {}

    def store(s, j, value):
        made[s, j] = value

    rows = flags.shape[0]
    shape = (rows, 128)
    flag = jnp.broadcast_to(flags, shape)
    octant = jnp.maximum(flag - 1, 0)
    kept = flag == 0
    bx = (octant >> 2) == 1
    by = (octant >> 1) & 1
    bz = octant & 1
    lane = iota(shape, 1)
    y = (lane >> 3) & 7
    z = lane & 7
    half = lane & 64
    low = lane < 64
    ya = 4 * by + (y >> 1)
    za = 4 * bz + (z >> 1)
    yb = jnp.clip(ya + 2 * (y & 1) - 1, 0, 7)
    zb = jnp.clip(za + 2 * (z & 1) - 1, 0, 7)
    index_ya = half + ya * 8 + z
    index_yb = half + yb * 8 + z
    index_za = half + y * 8 + za
    index_zb = half + y * 8 + zb
    index_plain = ya * 8 + za
    v = [load(0, j) for j in range(4)]
    w = [pltpu.roll(chunk, 64, 1) for chunk in v]
    v0 = jnp.where(bx, v[2], v[0])
    v1 = jnp.where(bx, v[3], v[1])
    w0 = jnp.where(bx, w[2], w[0])
    w1 = jnp.where(bx, w[3], w[1])
    before = jnp.where(bx, w[1], v[0])
    after = jnp.where(bx, v[3], w[2])
    near = (
        jnp.where(low, v0, w0),
        jnp.where(low, w0, v0),
        jnp.where(low, v1, w1),
        jnp.where(low, w1, v1),
    )
    far = (
        jnp.where(low, before, v0),
        jnp.where(low, v0, w1),
        jnp.where(low, w0, v1),
        jnp.where(low, v1, after),
    )
    for j in range(4):
        cur = 0.75 * near[j] + 0.25 * far[j]
        cur = 0.75 * lanes_of(cur, index_ya) + 0.25 * lanes_of(cur, index_yb)
        cur = 0.75 * lanes_of(cur, index_za) + 0.25 * lanes_of(cur, index_zb)
        store(0, j, jnp.where(kept, v[j], cur))
    for s in range(1, plain + 1):
        v = [load(s, j) for j in range(4)]
        for j in range(4):
            source = jnp.where(bx, v[2 + j // 2], v[j // 2])
            cur = lanes_of(source, index_plain + (j % 2) * 64)
            store(s, j, jnp.where(kept, v[j], cur))
    return made


def closure(h, alpha, n, cond):
    m = 1.0 - 1.0 / n
    log_x = jnp.log(alpha * jnp.maximum(-h, 0.0))
    log_up = m * jnp.log(1.0 + jnp.exp(n * log_x))
    root = jnp.exp(-0.5 * log_up)
    if cond is None:
        return root, None
    inner = 1.0 - jnp.exp((n - 1.0) * log_x - log_up)
    return root, cond * root * inner * inner


def kernel(
    peers,
    layers,
    head_hbm,
    water_prev_hbm,
    alpha_hbm,
    shape_n_hbm,
    theta_r_hbm,
    theta_s_hbm,
    sat_cond_hbm,
    refine_hbm,
    destination_hbm,
    neighbours_hbm,
    t_take_hbm,
    t_put_hbm,
    t_pool_hbm,
    results,
    head,
    water_prev,
    alpha,
    shape_n,
    theta_r,
    theta_s,
    sat_cond,
    refine,
    destination,
    neighbours,
    t_take,
    t_put,
    t_pool,
    load_sem,
    raw,
    sent_a,
    sent_b,
    got_a,
    got_b,
    work_a,
    work_b,
    place,
    settled_a,
    settled_b,
    own_hot,
    halo_hot,
    present,
    faces,
    ghosts,
    halo,
    ghost_planes,
    a_send,
    a_recv,
    b_send,
    b_recv,
    halo_send,
    halo_recv,
    plane_send,
    plane_recv,
):
    me = lax.axis_index("dom")
    level = lax.axis_index("depth")
    blocks = head.shape[1]
    both = 2 * blocks
    slots = 8 * peers
    shift = blocks.bit_length() - 1

    loads = []
    for source, target in (
        (destination_hbm, destination),
        (refine_hbm, refine),
        (head_hbm, head),
        (water_prev_hbm, water_prev),
        (alpha_hbm, alpha),
        (theta_r_hbm, theta_r),
        (shape_n_hbm, shape_n),
        (theta_s_hbm, theta_s),
        (sat_cond_hbm, sat_cond),
        (neighbours_hbm, neighbours),
        (t_take_hbm, t_take),
        (t_pool_hbm, t_pool),
        (t_put_hbm, t_put),
    ):
        loads.append(pltpu.make_async_copy(source, target, load_sem.at[len(loads)]))
    for copy in loads:
        copy.start()

    halo[...] = jnp.zeros_like(halo)
    ghost_planes[...] = jnp.zeros_like(ghost_planes)
    got_a[0] = jnp.zeros(got_a.shape[1:], F32)
    got_b[0] = jnp.zeros(got_b.shape[1:], F32)

    barrier = pltpu.get_barrier_semaphore()
    for k in range(1, peers):
        pl.semaphore_signal(
            barrier, inc=1, device_id=(lax.rem(me + k, peers), level), device_id_type=MESH
        )

    @pl.when(level > 0)
    def _():
        pl.semaphore_signal(barrier, inc=1, device_id=(me, level - 1), device_id_type=MESH)

    @pl.when(level < layers - 1)
    def _():
        pl.semaphore_signal(barrier, inc=1, device_id=(me, level + 1), device_id_type=MESH)

    for copy in loads[:9]:
        copy.wait()
    left = (head, alpha, shape_n, sat_cond)
    right = (water_prev, theta_r, theta_s)
    for s in range(4):
        cols = pl.ds(s * CELLS, CELLS)
        high, rest = split(left[s][0])
        raw[pl.ds(0, blocks), cols] = high
        raw[pl.ds(both, blocks), cols] = rest
        if s < 3:
            high, rest = split(right[s][0])
            raw[pl.ds(blocks, blocks), cols] = high
            raw[pl.ds(both + blocks, blocks), cols] = rest
        else:
            raw[pl.ds(blocks, blocks), cols] = jnp.zeros((blocks, CELLS), BF16)
            raw[pl.ds(both + blocks, blocks), cols] = jnp.zeros((blocks, CELLS), BF16)

    dest = jnp.concatenate([destination[...], destination[...]], axis=1)
    flag_row = jnp.concatenate([refine[...], refine[...]], axis=1)
    owner = dest >> shift
    spot = dest & (blocks - 1)
    shape = (blocks, both)
    own_lane = iota(shape, 1)
    own_row = iota(shape, 0)
    diagonal = own_lane == own_row
    owner_col = jnp.sum(jnp.where(diagonal, owner, 0), axis=1, keepdims=True)
    flag_col = jnp.sum(jnp.where(diagonal, flag_row, 0), axis=1, keepdims=True)
    earlier = (owner_col == owner) & (own_row < (own_lane & (blocks - 1)))
    rank = jnp.sum(earlier.astype(jnp.int32), axis=0, keepdims=True)
    shape = (slots, both)
    row = iota(shape, 0)
    side = (row >> 2) & 1
    target = me + (row >> 3)
    target = jnp.where(target >= peers, target - peers, target)
    chosen = (
        (side == (iota(shape, 1) >> shift))
        & (owner == target)
        & (rank == (row & 3))
        & (row >= 8)
    )
    hot = jnp.where(chosen, 1.0, 0.0)
    spot_sent = jnp.sum(hot * (spot + 1).astype(F32), axis=1, keepdims=True) - 1.0
    flag_sent = jnp.sum(hot * flag_row.astype(F32), axis=1, keepdims=True)
    hot = hot.astype(BF16)
    packed = dot(jnp.concatenate([hot, hot], axis=1), raw[...])
    filled = spot_sent >= 0.0
    for start in range(0, slots, 16):
        rows = slice(start, start + 16)
        made = adapt_rows(
            lambda s, j: packed[rows, s * CELLS + j * 128 : s * CELLS + (j + 1) * 128],
            flag_sent[rows].astype(jnp.int32),
            3,
        )
        upper = (iota((16, 128), 0) & 4) == 0
        peer = pl.ds(start // 8, 2)
        for j in range(4):
            conduct = closure(made[0, j], made[1, j], made[2, j], made[3, j])[1]
            conduct = jnp.where(filled[rows], conduct, 0.0)
            pair = jnp.where(upper, made[0, j], pltpu.roll(conduct, 4, 0))
            sent_a[peer, :, pl.ds(j * 128, 128)] = pair.reshape(2, 8, 128)
            for s, value in (
                (0, made[1, j]),
                (1, made[2, j]),
                (2, jnp.where(upper, made[3, j], made[0, j])),
            ):
                cols = pl.ds(s * CELLS + j * 128, 128)
                sent_b[peer, :, cols] = value.reshape(2, 8, 128)
        meta = jnp.broadcast_to(spot_sent[rows], (16, 128))
        sent_a[peer, :, pl.ds(CELLS, 128)] = meta.reshape(2, 8, 128)

    @pl.when((level > 0) & (level < layers - 1))
    def _():
        pl.semaphore_wait(barrier, peers + 1)

    @pl.when((level == 0) | (level == layers - 1))
    def _():
        pl.semaphore_wait(barrier, peers)

    moves_a = []
    moves_b = []
    for moves, source, target, gone, come in (
        (moves_a, sent_a, got_a, a_send, a_recv),
        (moves_b, sent_b, got_b, b_send, b_recv),
    ):
        for k in range(1, peers):
            moves.append(
                pltpu.make_async_remote_copy(
                    src_ref=source.at[k],
                    dst_ref=target.at[k],
                    send_sem=gone.at[k],
                    recv_sem=come.at[k],
                    device_id=(lax.rem(me + k, peers), level),
                    device_id_type=MESH,
                )
            )
    for copy in moves_a:
        copy.start()

    def put_rows(work, start, cols, value):
        high, rest = split(value)
        work[pl.ds(start, 16), cols] = high
        work[pl.ds(both + start, 16), cols] = rest

    for start in range(0, blocks, 16):
        made = adapt_rows(
            lambda s, j: left[s][0, pl.ds(start, 16), pl.ds(j * 128, 128)],
            flag_col[start : start + 16],
            3,
        )
        for j in range(4):
            conduct = closure(made[0, j], made[1, j], made[2, j], made[3, j])[1]
            put_rows(work_a, start, pl.ds(j * 128, 128), made[0, j])
            put_rows(work_a, blocks + start, pl.ds(j * 128, 128), conduct)
            for s in range(3):
                put_rows(work_b, start, pl.ds(s * CELLS + j * 128, 128), made[s + 1, j])
    shape = (both, both)
    wanted = (
        ((iota(shape, 0) & (blocks - 1)) == spot)
        & ((iota(shape, 0) >> shift) == (iota(shape, 1) >> shift))
        & (owner == me)
    )
    hot = jnp.where(wanted, 1.0, 0.0).astype(BF16)
    place[...] = jnp.concatenate([hot, hot], axis=1)
    settled_a[...] = dot(place[...], work_a[...])
    for copy in moves_b:
        copy.start()

    for copy in loads[9:]:
        copy.wait()
    eye = jnp.where(iota((blocks, blocks), 0) == iota((blocks, blocks), 1), 1.0, 0.0)
    shape = (blocks, 128)
    lane = iota(shape, 1)
    low = lane < 64
    for face in range(4):
        column = lax.dot_general(
            eye,
            neighbours[face].astype(F32),
            (((1,), (1,)), ((), ())),
            precision=lax.Precision.HIGHEST,
            preferred_element_type=F32,
        ).astype(jnp.int32)
        entry = [jnp.broadcast_to(column[:, e : e + 1], shape) for e in range(4)]
        full = entry[3] >= 0
        present[face] = jnp.where(entry[0] >= 0, 0.5, 0.0)
        wants = [jnp.where(full, -1, entry[0])] + [jnp.where(full, entry[e], -1) for e in range(4)]
        outer = []
        for number, want in enumerate(wants):
            gap = want - me * blocks
            listed = want >= 0
            hit = ((lane & (blocks - 1)) == gap) & listed
            own_hot[face, :, pl.ds(number * 128, 128)] = jnp.where(hit, 1.0, 0.0).astype(BF16)
            spot_out = jnp.where(gap < 0, gap + REACH, gap - blocks + REACH)
            hit = ((lane & (2 * REACH - 1)) == spot_out) & listed & ((gap < 0) | (gap >= blocks))
            outer.append(jnp.where(hit, 1.0, 0.0))
        outer.append(jnp.zeros(shape, F32))
        for number in range(3):
            value = jnp.where(low, outer[2 * number], outer[2 * number + 1])
            halo_hot[face, :, pl.ds(number * 128, 128)] = value.astype(BF16)
    low_on = jnp.where(level > 0, 0.5, 0.0)
    high_on = jnp.where(level < layers - 1, 0.5, 0.0)
    lane_q = iota((128, 128), 1)
    quarter = ((lane_q >> 5) & 1) * 2 + ((lane_q >> 2) & 1)
    masks = [jnp.where(quarter == e, 1.0, 0.0).astype(BF16) for e in range(4)]

    for copy in moves_a:
        copy.wait_recv()
    spot_got = got_a[:, :, pl.ds(CELLS, 128)].reshape(slots, 128)
    shape = (slots, both)
    row = iota(shape, 0)
    used = (
        ((iota(shape, 1) & (blocks - 1)).astype(F32) == spot_got)
        & ((iota(shape, 1) >> shift) == ((row >> 2) & 1))
        & (row >= 8)
    )
    hot = jnp.where(used, 1.0, 0.0).astype(BF16)
    used_hot = jnp.concatenate([hot, hot], axis=0)

    def scatter(value):
        return lax.dot_general(
            used_hot,
            jnp.concatenate(split(value), axis=0),
            (((0,), (0,)), ((), ())),
            preferred_element_type=F32,
        )

    settled_a[...] += scatter(got_a[:, :, pl.ds(0, CELLS)].reshape(slots, CELLS))

    top_rows = pl.ds(0, blocks)
    end_rows = pl.ds(blocks, blocks)
    seg = [pl.ds(s * CELLS, CELLS) for s in range(3)]
    lane_all = iota((blocks, CELLS), 1)

    def other_fields():
        for start in range(0, blocks, 16):
            made = adapt_rows(
                lambda s, j: right[s][0, pl.ds(start, 16), pl.ds(j * 128, 128)],
                flag_col[start : start + 16],
                2,
            )
            for j in range(4):
                for s, value in ((0, made[1, j]), (1, made[2, j]), (2, made[0, j])):
                    put_rows(work_b, blocks + start, pl.ds(s * CELLS + j * 128, 128), value)
        settled_b[...] = dot(place[...], work_b[...])
        for copy in moves_b:
            copy.wait_recv()
        settled_b[...] += scatter(got_b[...].reshape(slots, 3 * CELLS))

    def water_of(root):
        resid = settled_b[end_rows, seg[0]]
        return resid + (settled_b[end_rows, seg[1]] - resid) * root * root

    def gather_table(high, rest, pooled_high, pooled_rest):
        parts = [high, rest]
        for mask in masks:
            parts += [pooled_high * mask[: high.shape[0]], pooled_rest * mask[: high.shape[0]]]
        return parts

    def pool(stacked):
        high, rest = split(stacked)
        both_parts = dot(jnp.concatenate([high, rest], axis=0), t_pool[...])
        count = stacked.shape[0]
        pooled_high, pooled_rest = split(both_parts[:count] + both_parts[count:])
        return high, rest, pooled_high, pooled_rest

    opposite = (1, 0, 3, 2)

    def evaluate(step, h, conduct, meanwhile):
        terms = jnp.concatenate([*split(h), *split(conduct)], axis=0)
        taken = dot(terms, t_take[...])
        face_h = taken[:blocks] + taken[blocks:both]
        face_k = taken[both : both + blocks] + taken[both + blocks :]
        for chunk in range(3):
            part_h = face_h[:, chunk * 128 : chunk * 128 + 128]
            part_k = face_k[:, chunk * 128 : chunk * 128 + 128]
            faces[2 * chunk] = jnp.where(low, part_h, pltpu.roll(part_k, 64, 1))
            faces[2 * chunk + 1] = jnp.where(low, pltpu.roll(part_h, 64, 1), part_k)

        def halo_copy(side, way):
            start = 0 if side else blocks - REACH
            return pltpu.make_async_remote_copy(
                src_ref=faces.at[pl.ds(0, 4), pl.ds(start, REACH)],
                dst_ref=halo.at[step, side],
                send_sem=halo_send.at[step, side],
                recv_sem=halo_recv.at[step, side],
                device_id=(me + way, level),
                device_id_type=MESH,
            )

        def plane_copy(side, way):
            return pltpu.make_async_remote_copy(
                src_ref=faces.at[5 - side],
                dst_ref=ghost_planes.at[step, side],
                send_sem=plane_send.at[step, side],
                recv_sem=plane_recv.at[step, side],
                device_id=(me, level + way),
                device_id_type=MESH,
            )

        @pl.when(me < peers - 1)
        def _():
            halo_copy(0, 1).start()

        @pl.when(me > 0)
        def _():
            halo_copy(1, -1).start()

        @pl.when(level < layers - 1)
        def _():
            plane_copy(0, 1).start()

        @pl.when(level > 0)
        def _():
            plane_copy(1, -1).start()

        flux = jnp.zeros((blocks, CELLS), F32)
        total = jnp.zeros((blocks, CELLS), F32)
        for stride, rise in ((64, 0.0), (8, 0.0), (1, 1.0)):
            inside = (lane_all & (7 * stride)) < 7 * stride
            near_h = pltpu.roll(h, CELLS - stride, 1)
            near_k = pltpu.roll(conduct, CELLS - stride, 1)
            part = jnp.where(inside, 0.5 * (conduct + near_k), 0.0)
            gain = part * (near_h - h + rise)
            flux = flux + gain - pltpu.roll(gain, stride, 1)
            if step == 0:
                total = total + part + pltpu.roll(part, stride, 1)
        parts = pool(faces[pl.ds(0, 4)].reshape(4 * blocks, 128))
        for face in range(4):
            rows = slice(opposite[face] * blocks, (opposite[face] + 1) * blocks)
            table = gather_table(*[part[rows] for part in parts])
            ghosts[face] = dot(own_hot[face], jnp.concatenate(table, axis=0))
        resid, diag = meanwhile(flux, total)

        @pl.when(me < peers - 1)
        def _():
            halo_copy(0, 1).wait_send()
            halo_copy(1, -1).wait_recv()

        @pl.when(me > 0)
        def _():
            halo_copy(1, -1).wait_send()
            halo_copy(0, 1).wait_recv()

        @pl.when(level < layers - 1)
        def _():
            plane_copy(0, 1).wait_send()
            plane_copy(1, -1).wait_recv()

        @pl.when(level > 0)
        def _():
            plane_copy(1, -1).wait_send()
            plane_copy(0, 1).wait_recv()

        wide = 2 * REACH
        stacked = [halo[step, side, face] for face in range(4) for side in range(2)]
        parts = pool(jnp.concatenate(stacked, axis=0))
        spare = jnp.zeros((2 * wide, 128), BF16)
        sums = []
        gaps = []
        for face in range(4):
            rows = slice(opposite[face] * wide, (opposite[face] + 1) * wide)
            table = gather_table(*[part[rows] for part in parts]) + [spare]
            ghost = ghosts[face] + dot(halo_hot[face], jnp.concatenate(table, axis=0))
            sums.append(present[face] * (faces[face] + ghost))
            gaps.append(ghost - faces[face])
        for side, on, lift in ((0, low_on, -1.0), (1, high_on, 1.0)):
            ghost = ghost_planes[step, side]
            sums.append(on * (faces[4 + side] + ghost))
            gaps.append(ghost - faces[4 + side] + lift)
        push = []
        rim = []
        for first in range(0, 6, 2):
            here = pltpu.roll(sums[first], 64, 1)
            there = sums[first + 1]
            push.append(
                jnp.where(low, here * gaps[first], there * pltpu.roll(gaps[first + 1], 64, 1))
            )
            rim.append(jnp.where(low, here, there))
        push = jnp.concatenate(push, axis=1)
        rim = jnp.concatenate(rim, axis=1)
        if step == 0:
            spread = dot(jnp.concatenate([*split(push), *split(rim)], axis=0), t_put[...])
            diag = diag + spread[both : both + blocks] + spread[both + blocks :]
        else:
            spread = dot(jnp.concatenate(split(push), axis=0), t_put[...])
        return resid - (spread[:blocks] + spread[blocks:both]), diag

    start_head = settled_a[top_rows]

    def first_balance(flux, total):
        other_fields()
        alpha_here = settled_b[top_rows, seg[0]]
        n = settled_b[top_rows, seg[1]]
        root = closure(start_head, alpha_here, n, None)[0]
        resid = 4.0 * (water_of(root) - settled_b[end_rows, seg[2]]) - flux
        room = settled_b[end_rows, seg[1]] - settled_b[end_rows, seg[0]]
        return resid, 4.0 * room * alpha_here + total

    resid, diag = evaluate(0, start_head, settled_a[end_rows], first_balance)
    fresh = start_head - resid / diag
    results[top_rows] = fresh
    root, conduct = closure(
        fresh, settled_b[top_rows, seg[0]], settled_b[top_rows, seg[1]], settled_b[top_rows, seg[2]]
    )

    def second_balance(flux, total):
        return 4.0 * (water_of(root) - settled_b[end_rows, seg[2]]) - flux, None

    results[end_rows] = evaluate(1, fresh, conduct, second_balance)[0]
    for copy in moves_a + moves_b:
        copy.wait_send()


def on_device(
    peers,
    layers,
    head,
    water_prev,
    alpha,
    shape_n,
    theta_r,
    theta_s,
    sat_cond,
    refine,
    destination,
    neighbours,
):
    blocks = head.shape[1]
    both = 2 * blocks
    slots = 8 * peers
    table = take_table()
    vmem = pl.BlockSpec(memory_space=pltpu.VMEM)
    hbm = pl.BlockSpec(memory_space=pltpu.HBM)
    dma = pltpu.SemaphoreType.DMA
    results = pl.pallas_call(
        functools.partial(kernel, peers, layers),
        out_shape=jax.ShapeDtypeStruct((2 * blocks, CELLS), F32),
        in_specs=[hbm] * 13,
        out_specs=vmem,
        scratch_shapes=[pltpu.VMEM(head.shape, F32)] * 7
        + [
            pltpu.VMEM((1, blocks), jnp.int32),
            pltpu.VMEM((1, blocks), jnp.int32),
            pltpu.VMEM((4, 4, blocks), jnp.int32),
            pltpu.VMEM((CELLS, 384), BF16),
            pltpu.VMEM((384, CELLS), BF16),
            pltpu.VMEM((128, 128), BF16),
            dma((13,)),
            pltpu.VMEM((2 * both, 4 * CELLS), BF16),
            pltpu.VMEM((peers, 8, CELLS + 128), F32),
            pltpu.VMEM((peers, 8, 3 * CELLS), F32),
            pltpu.VMEM((peers, 8, CELLS + 128), F32),
            pltpu.VMEM((peers, 8, 3 * CELLS), F32),
            pltpu.VMEM((2 * both, CELLS), BF16),
            pltpu.VMEM((2 * both, 3 * CELLS), BF16),
            pltpu.VMEM((both, 2 * both), BF16),
            pltpu.VMEM((both, CELLS), F32),
            pltpu.VMEM((both, 3 * CELLS), F32),
            pltpu.VMEM((4, blocks, 640), BF16),
            pltpu.VMEM((4, blocks, 384), BF16),
            pltpu.VMEM((4, blocks, 128), F32),
            pltpu.VMEM((6, blocks, 128), F32),
            pltpu.VMEM((4, blocks, 128), F32),
            pltpu.VMEM((2, 2, 4, REACH, 128), F32),
            pltpu.VMEM((2, 2, blocks, 128), F32),
            dma((peers,)),
            dma((peers,)),
            dma((peers,)),
            dma((peers,)),
            dma((2, 2)),
            dma((2, 2)),
            dma((2, 2)),
            dma((2, 2)),
        ],
        compiler_params=pltpu.CompilerParams(
            collective_id=0, has_side_effects=True, vmem_limit_bytes=60 * 1024 * 1024
        ),
    )(
        head,
        water_prev,
        alpha,
        shape_n,
        theta_r,
        theta_s,
        sat_cond,
        refine.reshape(1, blocks),
        destination.reshape(1, blocks),
        neighbours.transpose(1, 2, 0),
        jnp.asarray(table, BF16),
        jnp.asarray(table.T, BF16),
        jnp.asarray(pool_table(), BF16),
    )
    return results[:blocks][None], results[blocks:][None]


def solution(mesh):
    cells = P("depth", "dom", None)
    placed = (cells,) * 7 + (P("dom"), P("dom"), P("dom", None, None))
    return jax.shard_map(
        functools.partial(on_device, mesh.shape["dom"], mesh.shape["depth"]),
        mesh=mesh,
        in_specs=placed,
        out_specs=(cells, cells),
        check_vma=False,
    )
```

```python
import functools

import jax
import jax.numpy as jnp
import numpy as np
from jax import lax
from jax.experimental import pallas as pl
from jax.experimental.pallas import tpu as pltpu
from jax.sharding import PartitionSpec as P

MESH = pl.DeviceIdType.MESH
CELLS = 512
CAP = 4
REACH = 16
F32 = jnp.float32
BF16 = jnp.bfloat16


def face_cells(face):
    listed = []
    for first in range(8):
        for second in range(8):
            listed.append(
                (
                    first * 8 + second,
                    448 + first * 8 + second,
                    first * 64 + second,
                    first * 64 + 56 + second,
                    first * 64 + second * 8,
                    first * 64 + second * 8 + 7,
                )[face]
            )
    return listed


def take_table():
    table = np.zeros((CELLS, 384), np.float32)
    for face in range(6):
        for spot, cell in enumerate(face_cells(face)):
            table[cell, face * 64 + spot] = 1.0
    return table


def pool_table():
    table = np.zeros((128, 128), np.float32)
    for half in range(2):
        for a in range(8):
            for b in range(8):
                for u in range(2):
                    for w in range(2):
                        source = (2 * (a % 4) + u) * 8 + 2 * (b % 4) + w
                        table[half * 64 + source, half * 64 + a * 8 + b] = 0.25
    return table


def iota(shape, axis):
    return lax.broadcasted_iota(jnp.int32, shape, axis)


def split(x):
    high = x.astype(BF16)
    return high, (x - high.astype(F32)).astype(BF16)


def dot(a, b):
    return jnp.dot(a, b, preferred_element_type=F32)


def lanes_of(x, index):
    return jnp.take_along_axis(x, index, axis=1, mode="promise_in_bounds")


def adapt_rows(load, flags, plain):
    made = {}

    def store(s, j, value):
        made[s, j] = value

    rows = flags.shape[0]
    shape = (rows, 128)
    flag = jnp.broadcast_to(flags, shape)
    octant = jnp.maximum(flag - 1, 0)
    kept = flag == 0
    bx = (octant >> 2) == 1
    by = (octant >> 1) & 1
    bz = octant & 1
    lane = iota(shape, 1)
    y = (lane >> 3) & 7
    z = lane & 7
    half = lane & 64
    low = lane < 64
    ya = 4 * by + (y >> 1)
    za = 4 * bz + (z >> 1)
    yb = jnp.clip(ya + 2 * (y & 1) - 1, 0, 7)
    zb = jnp.clip(za + 2 * (z & 1) - 1, 0, 7)
    index_ya = half + ya * 8 + z
    index_yb = half + yb * 8 + z
    index_za = half + y * 8 + za
    index_zb = half + y * 8 + zb
    index_plain = ya * 8 + za
    v = [load(0, j) for j in range(4)]
    w = [pltpu.roll(chunk, 64, 1) for chunk in v]
    v0 = jnp.where(bx, v[2], v[0])
    v1 = jnp.where(bx, v[3], v[1])
    w0 = jnp.where(bx, w[2], w[0])
    w1 = jnp.where(bx, w[3], w[1])
    before = jnp.where(bx, w[1], v[0])
    after = jnp.where(bx, v[3], w[2])
    near = (
        jnp.where(low, v0, w0),
        jnp.where(low, w0, v0),
        jnp.where(low, v1, w1),
        jnp.where(low, w1, v1),
    )
    far = (
        jnp.where(low, before, v0),
        jnp.where(low, v0, w1),
        jnp.where(low, w0, v1),
        jnp.where(low, v1, after),
    )
    for j in range(4):
        cur = 0.75 * near[j] + 0.25 * far[j]
        cur = 0.75 * lanes_of(cur, index_ya) + 0.25 * lanes_of(cur, index_yb)
        cur = 0.75 * lanes_of(cur, index_za) + 0.25 * lanes_of(cur, index_zb)
        store(0, j, jnp.where(kept, v[j], cur))
    for s in range(1, plain + 1):
        v = [load(s, j) for j in range(4)]
        for j in range(4):
            source = jnp.where(bx, v[2 + j // 2], v[j // 2])
            cur = lanes_of(source, index_plain + (j % 2) * 64)
            store(s, j, jnp.where(kept, v[j], cur))
    return made


def closure(h, alpha, n, cond):
    m = 1.0 - 1.0 / n
    log_x = jnp.log(alpha * jnp.maximum(-h, 0.0))
    log_up = m * jnp.log(1.0 + jnp.exp(n * log_x))
    root = jnp.exp(-0.5 * log_up)
    if cond is None:
        return root, None
    inner = 1.0 - jnp.exp((n - 1.0) * log_x - log_up)
    return root, cond * root * inner * inner


def kernel(
    peers,
    layers,
    head_hbm,
    water_prev_hbm,
    alpha_hbm,
    shape_n_hbm,
    theta_r_hbm,
    theta_s_hbm,
    sat_cond_hbm,
    refine_hbm,
    destination_hbm,
    neighbours_hbm,
    t_take_hbm,
    t_put_hbm,
    t_pool_hbm,
    results,
    head,
    water_prev,
    alpha,
    shape_n,
    theta_r,
    theta_s,
    sat_cond,
    refine,
    destination,
    neighbours,
    t_take,
    t_put,
    t_pool,
    load_sem,
    raw,
    sent_a,
    sent_b,
    got_a,
    got_b,
    work_a,
    work_b,
    place,
    settled_a,
    settled_b,
    own_hot,
    halo_hot,
    present,
    faces,
    ghosts,
    halo,
    ghost_planes,
    a_send,
    a_recv,
    b_send,
    b_recv,
    halo_send,
    halo_recv,
    plane_send,
    plane_recv,
):
    me = lax.axis_index("dom")
    level = lax.axis_index("depth")
    blocks = head.shape[1]
    both = 2 * blocks
    slots = 8 * peers
    shift = blocks.bit_length() - 1

    loads = []
    for source, target in (
        (destination_hbm, destination),
        (refine_hbm, refine),
        (head_hbm, head),
        (water_prev_hbm, water_prev),
        (alpha_hbm, alpha),
        (theta_r_hbm, theta_r),
        (shape_n_hbm, shape_n),
        (theta_s_hbm, theta_s),
        (sat_cond_hbm, sat_cond),
        (neighbours_hbm, neighbours),
        (t_take_hbm, t_take),
        (t_pool_hbm, t_pool),
        (t_put_hbm, t_put),
    ):
        loads.append(pltpu.make_async_copy(source, target, load_sem.at[len(loads)]))
    for copy in loads:
        copy.start()

    halo[...] = jnp.zeros_like(halo)
    ghost_planes[...] = jnp.zeros_like(ghost_planes)
    got_a[0] = jnp.zeros(got_a.shape[1:], F32)
    got_b[0] = jnp.zeros(got_b.shape[1:], F32)

    barrier = pltpu.get_barrier_semaphore()
    for k in range(1, peers):
        pl.semaphore_signal(
            barrier, inc=1, device_id=(lax.rem(me + k, peers), level), device_id_type=MESH
        )

    @pl.when(level > 0)
    def _():
        pl.semaphore_signal(barrier, inc=1, device_id=(me, level - 1), device_id_type=MESH)

    @pl.when(level < layers - 1)
    def _():
        pl.semaphore_signal(barrier, inc=1, device_id=(me, level + 1), device_id_type=MESH)

    for copy in loads[:2]:
        copy.wait()
    dest = jnp.concatenate([destination[...], destination[...]], axis=1)
    flag_row = jnp.concatenate([refine[...], refine[...]], axis=1)
    owner = dest >> shift
    spot = dest & (blocks - 1)
    shape = (blocks, both)
    own_lane = iota(shape, 1)
    own_row = iota(shape, 0)
    diagonal = own_lane == own_row
    owner_col = jnp.sum(jnp.where(diagonal, owner, 0), axis=1, keepdims=True)
    flag_col = jnp.sum(jnp.where(diagonal, flag_row, 0), axis=1, keepdims=True)
    earlier = (owner_col == owner) & (own_row < (own_lane & (blocks - 1)))
    rank = jnp.sum(earlier.astype(jnp.int32), axis=0, keepdims=True)
    shape = (slots, both)
    row = iota(shape, 0)
    side = (row >> 2) & 1
    target = me + (row >> 3)
    target = jnp.where(target >= peers, target - peers, target)
    chosen = (
        (side == (iota(shape, 1) >> shift))
        & (owner == target)
        & (rank == (row & 3))
        & (row >= 8)
    )
    hot = jnp.where(chosen, 1.0, 0.0)
    spot_sent = jnp.sum(hot * (spot + 1).astype(F32), axis=1, keepdims=True) - 1.0
    flag_sent = jnp.sum(hot * flag_row.astype(F32), axis=1, keepdims=True)
    hot = hot.astype(BF16)
    for copy in loads[2:9]:
        copy.wait()
    left = (head, alpha, shape_n, sat_cond)
    right = (water_prev, theta_r, theta_s)
    for s in range(4):
        cols = pl.ds(s * CELLS, CELLS)
        high, rest = split(left[s][0])
        raw[pl.ds(0, blocks), cols] = high
        raw[pl.ds(both, blocks), cols] = rest
        if s < 3:
            high, rest = split(right[s][0])
            raw[pl.ds(blocks, blocks), cols] = high
            raw[pl.ds(both + blocks, blocks), cols] = rest
        else:
            raw[pl.ds(blocks, blocks), cols] = jnp.zeros((blocks, CELLS), BF16)
            raw[pl.ds(both + blocks, blocks), cols] = jnp.zeros((blocks, CELLS), BF16)

    packed = dot(jnp.concatenate([hot, hot], axis=1), raw[...])
    filled = spot_sent >= 0.0
    for start in range(0, slots, 16):
        rows = slice(start, start + 16)
        made = adapt_rows(
            lambda s, j: packed[rows, s * CELLS + j * 128 : s * CELLS + (j + 1) * 128],
            flag_sent[rows].astype(jnp.int32),
            3,
        )
        upper = (iota((16, 128), 0) & 4) == 0
        peer = pl.ds(start // 8, 2)
        for j in range(4):
            conduct = closure(made[0, j], made[1, j], made[2, j], made[3, j])[1]
            conduct = jnp.where(filled[rows], conduct, 0.0)
            pair = jnp.where(upper, made[0, j], pltpu.roll(conduct, 4, 0))
            sent_a[peer, :, pl.ds(j * 128, 128)] = pair.reshape(2, 8, 128)
            for s, value in (
                (0, made[1, j]),
                (1, made[2, j]),
                (2, jnp.where(upper, made[3, j], made[0, j])),
            ):
                cols = pl.ds(s * CELLS + j * 128, 128)
                sent_b[peer, :, cols] = value.reshape(2, 8, 128)
        meta = jnp.broadcast_to(spot_sent[rows], (16, 128))
        sent_a[peer, :, pl.ds(CELLS, 128)] = meta.reshape(2, 8, 128)

    @pl.when((level > 0) & (level < layers - 1))
    def _():
        pl.semaphore_wait(barrier, peers + 1)

    @pl.when((level == 0) | (level == layers - 1))
    def _():
        pl.semaphore_wait(barrier, peers)

    moves_a = []
    moves_b = []
    for moves, source, target, gone, come in (
        (moves_a, sent_a, got_a, a_send, a_recv),
        (moves_b, sent_b, got_b, b_send, b_recv),
    ):
        for k in range(1, peers):
            moves.append(
                pltpu.make_async_remote_copy(
                    src_ref=source.at[k],
                    dst_ref=target.at[k],
                    send_sem=gone.at[k],
                    recv_sem=come.at[k],
                    device_id=(lax.rem(me + k, peers), level),
                    device_id_type=MESH,
                )
            )
    for copy in moves_a:
        copy.start()

    def put_rows(work, start, cols, value):
        high, rest = split(value)
        work[pl.ds(start, 16), cols] = high
        work[pl.ds(both + start, 16), cols] = rest

    for start in range(0, blocks, 16):
        made = adapt_rows(
            lambda s, j: left[s][0, pl.ds(start, 16), pl.ds(j * 128, 128)],
            flag_col[start : start + 16],
            3,
        )
        for j in range(4):
            conduct = closure(made[0, j], made[1, j], made[2, j], made[3, j])[1]
            put_rows(work_a, start, pl.ds(j * 128, 128), made[0, j])
            put_rows(work_a, blocks + start, pl.ds(j * 128, 128), conduct)
            for s in range(3):
                put_rows(work_b, start, pl.ds(s * CELLS + j * 128, 128), made[s + 1, j])
    shape = (both, both)
    wanted = (
        ((iota(shape, 0) & (blocks - 1)) == spot)
        & ((iota(shape, 0) >> shift) == (iota(shape, 1) >> shift))
        & (owner == me)
    )
    hot = jnp.where(wanted, 1.0, 0.0).astype(BF16)
    place[...] = jnp.concatenate([hot, hot], axis=1)
    settled_a[...] = dot(place[...], work_a[...])
    for copy in moves_b:
        copy.start()

    for copy in loads[9:]:
        copy.wait()
    eye = jnp.where(iota((blocks, blocks), 0) == iota((blocks, blocks), 1), 1.0, 0.0)
    shape = (blocks, 128)
    lane = iota(shape, 1)
    low = lane < 64
    for face in range(4):
        column = lax.dot_general(
            eye,
            neighbours[face].astype(F32),
            (((1,), (1,)), ((), ())),
            precision=lax.Precision.HIGHEST,
            preferred_element_type=F32,
        ).astype(jnp.int32)
        entry = [jnp.broadcast_to(column[:, e : e + 1], shape) for e in range(4)]
        full = entry[3] >= 0
        present[face] = jnp.where(entry[0] >= 0, 0.5, 0.0)
        wants = [jnp.where(full, -1, entry[0])] + [jnp.where(full, entry[e], -1) for e in range(4)]
        outer = []
        for number, want in enumerate(wants):
            gap = want - me * blocks
            listed = want >= 0
            hit = ((lane & (blocks - 1)) == gap) & listed
            own_hot[face, :, pl.ds(number * 128, 128)] = jnp.where(hit, 1.0, 0.0).astype(BF16)
            spot_out = jnp.where(gap < 0, gap + REACH, gap - blocks + REACH)
            hit = ((lane & (2 * REACH - 1)) == spot_out) & listed & ((gap < 0) | (gap >= blocks))
            outer.append(jnp.where(hit, 1.0, 0.0))
        outer.append(jnp.zeros(shape, F32))
        for number in range(3):
            value = jnp.where(low, outer[2 * number], outer[2 * number + 1])
            halo_hot[face, :, pl.ds(number * 128, 128)] = value.astype(BF16)
    low_on = jnp.where(level > 0, 0.5, 0.0)
    high_on = jnp.where(level < layers - 1, 0.5, 0.0)
    lane_q = iota((128, 128), 1)
    quarter = ((lane_q >> 5) & 1) * 2 + ((lane_q >> 2) & 1)
    masks = [jnp.where(quarter == e, 1.0, 0.0).astype(BF16) for e in range(4)]

    for copy in moves_a:
        copy.wait_recv()
    spot_got = got_a[:, :, pl.ds(CELLS, 128)].reshape(slots, 128)
    shape = (slots, both)
    row = iota(shape, 0)
    used = (
        ((iota(shape, 1) & (blocks - 1)).astype(F32) == spot_got)
        & ((iota(shape, 1) >> shift) == ((row >> 2) & 1))
        & (row >= 8)
    )
    hot = jnp.where(used, 1.0, 0.0).astype(BF16)
    used_hot = jnp.concatenate([hot, hot], axis=0)

    def scatter(value):
        return lax.dot_general(
            used_hot,
            jnp.concatenate(split(value), axis=0),
            (((0,), (0,)), ((), ())),
            preferred_element_type=F32,
        )

    settled_a[...] += scatter(got_a[:, :, pl.ds(0, CELLS)].reshape(slots, CELLS))

    top_rows = pl.ds(0, blocks)
    end_rows = pl.ds(blocks, blocks)
    seg = [pl.ds(s * CELLS, CELLS) for s in range(3)]
    lane_all = iota((blocks, CELLS), 1)

    def other_fields():
        for start in range(0, blocks, 16):
            made = adapt_rows(
                lambda s, j: right[s][0, pl.ds(start, 16), pl.ds(j * 128, 128)],
                flag_col[start : start + 16],
                2,
            )
            for j in range(4):
                for s, value in ((0, made[1, j]), (1, made[2, j]), (2, made[0, j])):
                    put_rows(work_b, blocks + start, pl.ds(s * CELLS + j * 128, 128), value)
        settled_b[...] = dot(place[...], work_b[...])
        for copy in moves_b:
            copy.wait_recv()
        settled_b[...] += scatter(got_b[...].reshape(slots, 3 * CELLS))

    def water_of(root):
        resid = settled_b[end_rows, seg[0]]
        return resid + (settled_b[end_rows, seg[1]] - resid) * root * root

    def gather_table(high, rest, pooled_high, pooled_rest):
        parts = [high, rest]
        for mask in masks:
            parts += [pooled_high * mask[: high.shape[0]], pooled_rest * mask[: high.shape[0]]]
        return parts

    def pool(stacked):
        high, rest = split(stacked)
        both_parts = dot(jnp.concatenate([high, rest], axis=0), t_pool[...])
        count = stacked.shape[0]
        pooled_high, pooled_rest = split(both_parts[:count] + both_parts[count:])
        return high, rest, pooled_high, pooled_rest

    opposite = (1, 0, 3, 2)

    def evaluate(step, h, conduct, meanwhile):
        terms = jnp.concatenate([*split(h), *split(conduct)], axis=0)
        taken = dot(terms, t_take[...])
        face_h = taken[:blocks] + taken[blocks:both]
        face_k = taken[both : both + blocks] + taken[both + blocks :]
        for chunk in range(3):
            part_h = face_h[:, chunk * 128 : chunk * 128 + 128]
            part_k = face_k[:, chunk * 128 : chunk * 128 + 128]
            faces[2 * chunk] = jnp.where(low, part_h, pltpu.roll(part_k, 64, 1))
            faces[2 * chunk + 1] = jnp.where(low, pltpu.roll(part_h, 64, 1), part_k)

        def halo_copy(side, way):
            start = 0 if side else blocks - REACH
            return pltpu.make_async_remote_copy(
                src_ref=faces.at[pl.ds(0, 4), pl.ds(start, REACH)],
                dst_ref=halo.at[step, side],
                send_sem=halo_send.at[step, side],
                recv_sem=halo_recv.at[step, side],
                device_id=(me + way, level),
                device_id_type=MESH,
            )

        def plane_copy(side, way):
            return pltpu.make_async_remote_copy(
                src_ref=faces.at[5 - side],
                dst_ref=ghost_planes.at[step, side],
                send_sem=plane_send.at[step, side],
                recv_sem=plane_recv.at[step, side],
                device_id=(me, level + way),
                device_id_type=MESH,
            )

        @pl.when(me < peers - 1)
        def _():
            halo_copy(0, 1).start()

        @pl.when(me > 0)
        def _():
            halo_copy(1, -1).start()

        @pl.when(level < layers - 1)
        def _():
            plane_copy(0, 1).start()

        @pl.when(level > 0)
        def _():
            plane_copy(1, -1).start()

        flux = jnp.zeros((blocks, CELLS), F32)
        total = jnp.zeros((blocks, CELLS), F32)
        for stride, rise in ((64, 0.0), (8, 0.0), (1, 1.0)):
            inside = (lane_all & (7 * stride)) < 7 * stride
            near_h = pltpu.roll(h, CELLS - stride, 1)
            near_k = pltpu.roll(conduct, CELLS - stride, 1)
            part = jnp.where(inside, 0.5 * (conduct + near_k), 0.0)
            gain = part * (near_h - h + rise)
            flux = flux + gain - pltpu.roll(gain, stride, 1)
            if step == 0:
                total = total + part + pltpu.roll(part, stride, 1)
        parts = pool(faces[pl.ds(0, 4)].reshape(4 * blocks, 128))
        for face in range(4):
            rows = slice(opposite[face] * blocks, (opposite[face] + 1) * blocks)
            table = gather_table(*[part[rows] for part in parts])
            ghosts[face] = dot(own_hot[face], jnp.concatenate(table, axis=0))
        resid, diag = meanwhile(flux, total)

        @pl.when(me < peers - 1)
        def _():
            halo_copy(1, -1).wait_recv()

        @pl.when(me > 0)
        def _():
            halo_copy(0, 1).wait_recv()

        wide = 2 * REACH
        stacked = [halo[step, side, face] for face in range(4) for side in range(2)]
        parts = pool(jnp.concatenate(stacked, axis=0))
        spare = jnp.zeros((2 * wide, 128), BF16)
        sums = []
        gaps = []
        for face in range(4):
            rows = slice(opposite[face] * wide, (opposite[face] + 1) * wide)
            table = gather_table(*[part[rows] for part in parts]) + [spare]
            ghost = ghosts[face] + dot(halo_hot[face], jnp.concatenate(table, axis=0))
            sums.append(present[face] * (faces[face] + ghost))
            gaps.append(ghost - faces[face])

        @pl.when(level < layers - 1)
        def _():
            plane_copy(1, -1).wait_recv()

        @pl.when(level > 0)
        def _():
            plane_copy(0, 1).wait_recv()

        for side, on, lift in ((0, low_on, -1.0), (1, high_on, 1.0)):
            ghost = ghost_planes[step, side]
            sums.append(on * (faces[4 + side] + ghost))
            gaps.append(ghost - faces[4 + side] + lift)
        push = []
        rim = []
        for first in range(0, 6, 2):
            here = pltpu.roll(sums[first], 64, 1)
            there = sums[first + 1]
            push.append(
                jnp.where(low, here * gaps[first], there * pltpu.roll(gaps[first + 1], 64, 1))
            )
            rim.append(jnp.where(low, here, there))
        push = jnp.concatenate(push, axis=1)
        rim = jnp.concatenate(rim, axis=1)
        if step == 0:
            spread = dot(jnp.concatenate([*split(push), *split(rim)], axis=0), t_put[...])
            diag = diag + spread[both : both + blocks] + spread[both + blocks :]
        else:
            spread = dot(jnp.concatenate(split(push), axis=0), t_put[...])

        @pl.when(me < peers - 1)
        def _():
            halo_copy(0, 1).wait_send()

        @pl.when(me > 0)
        def _():
            halo_copy(1, -1).wait_send()

        @pl.when(level < layers - 1)
        def _():
            plane_copy(0, 1).wait_send()

        @pl.when(level > 0)
        def _():
            plane_copy(1, -1).wait_send()

        return resid - (spread[:blocks] + spread[blocks:both]), diag

    start_head = settled_a[top_rows]

    def first_balance(flux, total):
        other_fields()
        alpha_here = settled_b[top_rows, seg[0]]
        n = settled_b[top_rows, seg[1]]
        root = closure(start_head, alpha_here, n, None)[0]
        resid = 4.0 * (water_of(root) - settled_b[end_rows, seg[2]]) - flux
        room = settled_b[end_rows, seg[1]] - settled_b[end_rows, seg[0]]
        return resid, 4.0 * room * alpha_here + total

    resid, diag = evaluate(0, start_head, settled_a[end_rows], first_balance)
    fresh = start_head - resid / diag
    results[top_rows] = fresh
    root, conduct = closure(
        fresh, settled_b[top_rows, seg[0]], settled_b[top_rows, seg[1]], settled_b[top_rows, seg[2]]
    )

    def second_balance(flux, total):
        return 4.0 * (water_of(root) - settled_b[end_rows, seg[2]]) - flux, None

    results[end_rows] = evaluate(1, fresh, conduct, second_balance)[0]
    for copy in moves_a + moves_b:
        copy.wait_send()


def on_device(
    peers,
    layers,
    head,
    water_prev,
    alpha,
    shape_n,
    theta_r,
    theta_s,
    sat_cond,
    refine,
    destination,
    neighbours,
):
    blocks = head.shape[1]
    both = 2 * blocks
    slots = 8 * peers
    table = take_table()
    vmem = pl.BlockSpec(memory_space=pltpu.VMEM)
    hbm = pl.BlockSpec(memory_space=pltpu.HBM)
    dma = pltpu.SemaphoreType.DMA
    results = pl.pallas_call(
        functools.partial(kernel, peers, layers),
        out_shape=jax.ShapeDtypeStruct((2 * blocks, CELLS), F32),
        in_specs=[hbm] * 13,
        out_specs=vmem,
        scratch_shapes=[pltpu.VMEM(head.shape, F32)] * 7
        + [
            pltpu.VMEM((1, blocks), jnp.int32),
            pltpu.VMEM((1, blocks), jnp.int32),
            pltpu.VMEM((4, 4, blocks), jnp.int32),
            pltpu.VMEM((CELLS, 384), BF16),
            pltpu.VMEM((384, CELLS), BF16),
            pltpu.VMEM((128, 128), BF16),
            dma((13,)),
            pltpu.VMEM((2 * both, 4 * CELLS), BF16),
            pltpu.VMEM((peers, 8, CELLS + 128), F32),
            pltpu.VMEM((peers, 8, 3 * CELLS), F32),
            pltpu.VMEM((peers, 8, CELLS + 128), F32),
            pltpu.VMEM((peers, 8, 3 * CELLS), F32),
            pltpu.VMEM((2 * both, CELLS), BF16),
            pltpu.VMEM((2 * both, 3 * CELLS), BF16),
            pltpu.VMEM((both, 2 * both), BF16),
            pltpu.VMEM((both, CELLS), F32),
            pltpu.VMEM((both, 3 * CELLS), F32),
            pltpu.VMEM((4, blocks, 640), BF16),
            pltpu.VMEM((4, blocks, 384), BF16),
            pltpu.VMEM((4, blocks, 128), F32),
            pltpu.VMEM((6, blocks, 128), F32),
            pltpu.VMEM((4, blocks, 128), F32),
            pltpu.VMEM((2, 2, 4, REACH, 128), F32),
            pltpu.VMEM((2, 2, blocks, 128), F32),
            dma((peers,)),
            dma((peers,)),
            dma((peers,)),
            dma((peers,)),
            dma((2, 2)),
            dma((2, 2)),
            dma((2, 2)),
            dma((2, 2)),
        ],
        compiler_params=pltpu.CompilerParams(
            collective_id=0, has_side_effects=True, vmem_limit_bytes=60 * 1024 * 1024
        ),
    )(
        head,
        water_prev,
        alpha,
        shape_n,
        theta_r,
        theta_s,
        sat_cond,
        refine.reshape(1, blocks),
        destination.reshape(1, blocks),
        neighbours.transpose(1, 2, 0),
        jnp.asarray(table, BF16),
        jnp.asarray(table.T, BF16),
        jnp.asarray(pool_table(), BF16),
    )
    return results[:blocks][None], results[blocks:][None]


def solution(mesh):
    cells = P("depth", "dom", None)
    placed = (cells,) * 7 + (P("dom"), P("dom"), P("dom", None, None))
    return jax.shard_map(
        functools.partial(on_device, mesh.shape["dom"], mesh.shape["depth"]),
        mesh=mesh,
        in_specs=placed,
        out_specs=(cells, cells),
        check_vma=False,
    )
```
